256 devices in a mesh: dp: 32 (over y, z), fsdp: 8 (over x, core).
Axes of the slice: x: 4, y: 4, z: 8, core: 2. Of those that a mesh axis runs over, the one named last changes fastest.
Arguments:
- mixed_heads: bfloat16 [65536, 4096], P(('dp', 'fsdp')), may hold values from -6 to 6
- out_grads: bfloat16 [65536, 4608], P(('dp', 'fsdp')), may hold values from -60 to 60
- admit_counts: int32 [256], P(('dp', 'fsdp')), may hold values from 1 to 3, as said below
- lengths: int32 [256, 3], P(('dp', 'fsdp')), may hold values from 60 to 80, as said below
- gauss_noise: float32 [4096, 4608], P('dp', 'fsdp'), may hold values from -6000 to 6000
Outputs:
- grad_shard: float32 [4096, 4608], P('dp', 'fsdp')
The draws below stay inside these ranges and needn't reach their ends.
Inputs may be any that keep to these rules, and one draw needn't show every extreme that they name: `admit_counts`: A device at dp index i admits at most 2 + 2 i // 32 sequences. In every draw the devices of one fsdp index each admit that most, every sequence 80 tokens long, so the devices of one fsdp index together hold at most 6400 admitted tokens and some hold exactly that many. `lengths`: row e gives the token counts of device e's sequences in order; only the first admit_counts[e] entries are admitted, and these fill the first slots of the device's block.
All inputs are finite; a program needn't handle non-finite values.
Results may differ from the reference program's by a relative error of at most 0.00036.
Values may be sent and summed in bfloat16 or wider, within the bound.
A program may use at most 128 MiB of HBM per device.

```python
import jax
import jax.numpy as jnp
from jax import lax

D = 4608
TOK_DEV = 256
MAXSEQ = 3
MAXLEN = 80
CLIP = 360000
INNER = 4096
TOKENS = 65536
N_DP = 32
N_FSDP = 8


def chosen_group(key):
    return jax.random.randint(key, (), 0, N_FSDP)


def draw_admit_counts(key, part):
    chosen = chosen_group(key)
    key = jax.random.fold_in(key, 11)
    index = jnp.arange(N_DP * N_FSDP, dtype=jnp.int32)
    dp_index = index // N_FSDP
    fsdp_index = index % N_FSDP
    most = 2 + 2 * dp_index // N_DP
    extra = jax.random.randint(key, (N_DP * N_FSDP,), 0, 2)
    return jnp.where(fsdp_index == chosen, most, most - 1 + extra).astype(jnp.int32)


def draw_lengths(key, part):
    chosen = chosen_group(key)
    key = jax.random.fold_in(key, 12)
    index = jnp.arange(N_DP * N_FSDP, dtype=jnp.int32)
    fsdp_index = index % N_FSDP
    values = jax.random.randint(key, (N_DP * N_FSDP, MAXSEQ), 3 * MAXLEN // 4, MAXLEN + 1)
    return jnp.where(fsdp_index[:, None] == chosen, MAXLEN, values).astype(jnp.int32)


def shard_levels(stream_key, shape, cuts, least, high):
    def one(dim, blocks):
        draws = jax.random.uniform(jax.random.fold_in(jax.random.fold_in(stream_key, 6), dim), (blocks,), jnp.float32, least / len(cuts), high / len(cuts))
        return jnp.repeat(jnp.exp(draws), shape[dim] // blocks).reshape((-1,) + (1,) * (len(shape) - dim - 1))

    level = one(*cuts[0])
    for cut in cuts[1:]:
        level = level * one(*cut)
    return level


def gaussian(stream_key, dims, deviation, limit, pieces=(), held_as=jnp.bfloat16):
    factor_of = shard_levels(stream_key, dims, pieces, -0.22, 0.18) if pieces else 1.0
    entries = jax.random.normal(stream_key, dims, jnp.float32) * deviation * factor_of
    return jnp.minimum(jnp.maximum(entries, -limit), limit).astype(held_as)


def setup_inputs(seed: int = 0) -> dict:
    splits = jax.random.split(jax.random.key(seed), 6)
    return {
        "mixed_heads": gaussian(splits[0], (TOKENS, INNER), 1.0, 6.0, ((0, 256),)),
        "out_grads": gaussian(splits[1], (TOKENS, D), 10.0, 60.0, ((0, 256),)),
        "admit_counts": draw_admit_counts(jax.random.fold_in(splits[5], 71), 0),
        "lengths": draw_lengths(jax.random.fold_in(splits[5], 71), 0),
        "gauss_noise": gaussian(splits[4], (INNER, D), 1000.0, 6000.0, ((0, 32), (1, 8)), jnp.float32),
    }


def device_clip(block_in, block_grad, count, seq_lengths):
    act_gram = lax.dot_general(block_in, block_in, (((1,), (1,)), ((), ())), preferred_element_type=jnp.float32)
    grad_gram = lax.dot_general(block_grad, block_grad, (((1,), (1,)), ((), ())), preferred_element_type=jnp.float32)
    admitted_seq = jnp.arange(MAXSEQ, dtype=jnp.int32) < count
    used = jnp.where(admitted_seq, seq_lengths, 0).astype(jnp.int32)
    ends = jnp.cumsum(used).astype(jnp.int32)
    starts = ends - used
    positions = jnp.arange(block_in.shape[0], dtype=jnp.int32)
    member = ((positions[None, :] >= starts[:, None]) & (positions[None, :] < ends[:, None])).astype(jnp.float32)
    product = act_gram * grad_gram
    spread = jnp.dot(member, product, precision=lax.Precision.HIGHEST)
    norm_sq = lax.optimization_barrier(jnp.sum(spread * member, axis=1))
    factor = CLIP / jnp.maximum(jnp.sqrt(norm_sq), jnp.float32(CLIP))
    row_factor = lax.optimization_barrier(jnp.sum(member * factor[:, None], axis=0))
    return (row_factor[:, None] * block_grad.astype(jnp.float32)).astype(jnp.bfloat16)

def reference(mixed_heads, out_grads, admit_counts, lengths, gauss_noise):
    devices = N_DP * N_FSDP
    blocks_in = mixed_heads.reshape(devices, TOK_DEV, mixed_heads.shape[1])
    blocks_grad = out_grads.reshape(devices, TOK_DEV, out_grads.shape[1])

    def one_device(items):
        return device_clip(items[0], items[1], items[2], items[3])
    clipped = lax.map(one_device, (blocks_in, blocks_grad, admit_counts, lengths))
    clipped = clipped.reshape(out_grads.shape)
    summed = lax.dot_general(mixed_heads, clipped, (((0,), (0,)), ((), ())), preferred_element_type=jnp.float32)
    admitted = jnp.sum(admit_counts).astype(jnp.float32)
    return (summed + gauss_noise) / admitted
```

```python
import functools

import jax
import jax.numpy as jnp
from jax import lax
from jax.experimental import pallas as pl
from jax.experimental.pallas import tpu as pltpu
from jax.sharding import PartitionSpec as P

MAXSEQ = 3
CLIP = 360000
MESH = pl.DeviceIdType.MESH
NX, NY, NZ = 4, 4, 8
ROWS = 240
CUT = 112
BLOCK = 128
CHUNK = NY * BLOCK
HALF = BLOCK // 2
QUARTER = 1152
PAD = 640
F32 = jnp.float32


def quantise(value):
    top = jnp.maximum(jnp.max(jnp.abs(value), axis=0, keepdims=True), 1e-30)
    code = jnp.round(value * (32767.0 / top)).astype(jnp.int32).astype(jnp.int16)
    return code, top * (1.0 / 32767.0)


def restore(code, scale):
    return code.astype(jnp.int32).astype(F32) * scale


def kernel(
    count_ref, lengths_ref, x_hbm, g_hbm, noise_ref, out_ref,
    xs, graw, gcut, gs, acc, away, near, total, ysend, yscale, yrecv, yrscale,
    zsend, zscale, zrecv, zrscale, fin_send, fin_recv, tally,
    load_sem, g_sem, xsend_sem, xrecv_sem, gsend_sem, grecv_sem, dsend_sem, drecv_sem,
    ysend_sem, yrecv_sem, ysend2_sem, yrecv2_sem, zsend_sem, zrecv_sem, zsend2_sem, zrecv2_sem,
    fsend_sem, frecv_sem, csend_sem, crecv_sem,
):
    dp = lax.axis_index("dp")
    fs = lax.axis_index("fsdp")
    x, core = fs // 2, fs % 2
    y, z = dp // NZ, dp % NZ

    def device(dx=0, dy=0, dz=0, dc=0):
        return (
            lax.rem(y + dy, NY) * NZ + lax.rem(z + dz, NZ),
            lax.rem(x + dx, NX) * 2 + lax.rem(core + dc, 2),
        )

    partners = (
        [device(dx=d) for d in (1, 2, 3)]
        + [device(dy=d) for d in (1, 2, 3)]
        + [device(dz=d) for d in range(1, NZ)]
        + [device(dc=1)]
    )
    barrier = pltpu.get_barrier_semaphore()
    for partner in partners:
        pl.semaphore_signal(barrier, inc=1, device_id=partner, device_id_type=MESH)

    def target(t):
        return lax.rem(z + 1 + t, NZ)

    def load(t, j):
        at = pl.multiple_of((j * NZ + target(t)) * BLOCK, BLOCK)
        return pltpu.make_async_copy(
            x_hbm.at[pl.ds(0, ROWS), pl.ds(at, BLOCK)],
            xs.at[t, pl.ds(0, ROWS), pl.ds(j * BLOCK, BLOCK)],
            load_sem.at[t, j],
        )

    def remote(src, dst, send, recv, to):
        return pltpu.make_async_remote_copy(
            src_ref=src, dst_ref=dst, send_sem=send, recv_sem=recv, device_id=to, device_id_type=MESH
        )

    def x_copy(t, k):
        if k == 0:
            src, dst, to = pl.ds(0, ROWS), pl.ds(ROWS, ROWS), device(dx=1)
        elif k == 1:
            src, dst, to = pl.ds(0, ROWS), pl.ds(2 * ROWS, ROWS), device(dx=3)
        elif k == 2:
            src, dst, to = pl.ds(ROWS, CUT), pl.ds(3 * ROWS, CUT), device(dx=1)
        else:
            src, dst, to = pl.ds(2 * ROWS + CUT, ROWS - CUT), pl.ds(3 * ROWS + CUT, ROWS - CUT), device(dx=3)
        return remote(xs.at[t, src], xs.at[t, dst], xsend_sem.at[t, k], xrecv_sem.at[t, k], to)

    def g_copy(k):
        d = (1, 3, 2)[k]
        return remote(
            gcut.at[lax.rem(x + d, NX)], gs.at[pl.ds((k + 1) * ROWS, ROWS)], gsend_sem.at[k], grecv_sem.at[k], device(dx=d)
        )

    def d_copy(t):
        return remote(away.at[t], near.at[t], dsend_sem.at[t], drecv_sem.at[t], device(dc=1))

    def y_copy(t, k):
        to = device(dy=k + 1)
        return (
            remote(ysend.at[t, k], yrecv.at[t, k], ysend_sem.at[t, k], yrecv_sem.at[t, k], to),
            remote(yscale.at[t, k], yrscale.at[t, k], ysend2_sem.at[t, k], yrecv2_sem.at[t, k], to),
        )

    def z_copy(t):
        to = device(dz=t + 1)
        return (
            remote(zsend.at[t], zrecv.at[t], zsend_sem.at[t], zrecv_sem.at[t], to),
            remote(zscale.at[t], zrscale.at[t], zsend2_sem.at[t], zrecv2_sem.at[t], to),
        )

    stages = (("dc", (1,)), ("dx", (1, 2, 3)), ("dy", (1, 2, 3)), ("dz", tuple(range(1, NZ))))
    first = (0, 1, 4, 7, 14)

    def c_copy(stage, i):
        axis, steps = stages[stage]
        slot = first[stage] + i
        return remote(
            tally.at[0, stage], tally.at[1, slot], csend_sem.at[slot], crecv_sem.at[slot], device(**{axis: steps[i]})
        )

    def count_send(stage):
        for i in range(len(stages[stage][1])):
            c_copy(stage, i).start()

    def count_take(stage):
        value = tally[0, stage]
        for i in range(len(stages[stage][1])):
            c_copy(stage, i).wait()
            value = value + tally[1, first[stage] + i]
        return value

    for t in range(NZ):
        for j in range(NY):
            load(t, j).start()
    g_load = pltpu.make_async_copy(g_hbm.at[pl.ds(0, ROWS)], graw, g_sem)
    g_load.start()
    tally[0, 0] = jnp.full((8, 128), count_ref[0], jnp.int32)

    pl.semaphore_wait(barrier, len(partners))

    for t in range(2):
        for j in range(NY):
            load(t, j).wait()
        x_copy(t, 0).start()
        x_copy(t, 1).start()
    count_send(0)

    for t in range(2, NZ):
        for j in range(NY):
            load(t, j).wait()
    own = xs[0, pl.ds(0, ROWS)]
    act = lax.dot_general(own, own, (((1,), (1,)), ((), ())), preferred_element_type=F32)
    for t in range(1, NZ):
        own = xs[t, pl.ds(0, ROWS)]
        act += lax.dot_general(own, own, (((1,), (1,)), ((), ())), preferred_element_type=F32)
    g_load.wait()
    grad = jnp.zeros((ROWS, ROWS), F32)
    for q in range(NX):
        part = graw[:, pl.ds(q * QUARTER, QUARTER)]
        grad += lax.dot_general(part, part, (((1,), (1,)), ((), ())), preferred_element_type=F32)
    product = act * grad
    row = lax.broadcasted_iota(jnp.int32, (ROWS, ROWS), 0)
    col = lax.broadcasted_iota(jnp.int32, (ROWS, ROWS), 1)
    line = lax.broadcasted_iota(jnp.int32, (ROWS, 1), 0)
    scale = jnp.zeros((ROWS, 1), F32)
    start = jnp.int32(0)
    for j in range(MAXSEQ):
        used = jnp.where(j < count_ref[0], lengths_ref[0, j], 0)
        end = start + used
        both = (row >= start) & (row < end) & (col >= start) & (col < end)
        sums = jnp.sum(jnp.where(both, product, 0.0), axis=1, keepdims=True)
        norm_sq = jnp.sum(sums, axis=0, keepdims=True)
        factor = CLIP / jnp.maximum(jnp.sqrt(norm_sq), F32(CLIP))
        scale = jnp.where((line >= start) & (line < end), factor, scale)
        start = end
    for q in range(NX):
        gcut[q] = (scale * graw[:, pl.ds(q * QUARTER, QUARTER)].astype(F32)).astype(jnp.bfloat16)
    for k in range(3):
        g_copy(k).start()
    gs[pl.ds(0, ROWS)] = gcut[x]

    def step(i, carry):
        @pl.when(i + 2 < NZ)
        def _():
            x_copy(i + 2, 0).start()
            x_copy(i + 2, 1).start()

        @pl.when(i < NZ)
        def _():
            x_copy(i, 0).wait_recv()
            x_copy(i, 1).wait_recv()
            x_copy(i, 2).start()
            x_copy(i, 3).start()

        @pl.when(i == 0)
        def _():
            for k in range(3):
                g_copy(k).wait()

        @pl.when((i >= 1) & (i < NZ + 1))
        def _():
            t = i - 1
            x_copy(t, 2).wait_recv()
            x_copy(t, 3).wait_recv()
            for pair in range(NY // 2):
                tile = lax.dot_general(
                    xs[t, :, pl.ds(pair * 2 * BLOCK, 2 * BLOCK)], gs[...], (((0,), (0,)), ((), ())),
                    preferred_element_type=F32,
                )
                for k in range(2):
                    for h in range(2):
                        acc[h, 2 * pair + k] = tile[k * BLOCK + h * HALF : k * BLOCK + (h + 1) * HALF]
            away[t] = acc[1 - core]
            total[t] = acc[core]
            d_copy(t).start()

        for stage in range(4):
            @pl.when(i == 2 * stage + 1)
            def _(stage=stage):
                value = count_take(stage)
                tally[0, stage + 1] = value
                if stage < 3:
                    count_send(stage + 1)

        @pl.when((i >= 2) & (i < NZ + 2))
        def _():
            t = i - 2
            d_copy(t).wait_recv()
            for k in range(3):
                to = lax.rem(y + k + 1, NY)
                code, factor = quantise(total[t, to] + near[t, to])
                ysend[t, k] = code
                yscale[t, k] = factor
                for copy in y_copy(t, k):
                    copy.start()

        @pl.when((i >= 3) & (i < NZ + 3))
        def _():
            t = i - 3
            value = total[t, y] + near[t, y]
            for k in range(3):
                for copy in y_copy(t, k):
                    copy.wait_recv()
                value += restore(yrecv[t, k], yrscale[t, k])

            @pl.when(t < NZ - 1)
            def _():
                code, factor = quantise(value)
                zsend[t] = code
                zscale[t] = factor
                for copy in z_copy(t):
                    copy.start()

            @pl.when(t == NZ - 1)
            def _():
                fin_send[...] = value

        return carry

    lax.fori_loop(0, NZ + 3, step, 0)

    value = fin_send[...]
    for t in range(NZ - 1):
        for copy in z_copy(t):
            copy.wait_recv()
        value += restore(zrecv[t], zrscale[t])
    fin_send[...] = value
    other = pl.multiple_of((1 - core) * (QUARTER - PAD), 128)
    last = remote(fin_send.at[:, pl.ds(other, PAD)], fin_recv, fsend_sem, frecv_sem, device(dc=1))
    last.start()
    admitted = tally[0, 4, 0:1, 0:1].astype(F32)

    def finish(c, part, rows):
        lo = c * (PAD - 576)
        out_ref[rows] = (part[:, lo : lo + 576] + noise_ref[rows]) / admitted

    for c in range(2):
        @pl.when(core == c)
        def _(c=c):
            mine = fin_send[:, c * (QUARTER - PAD) : c * (QUARTER - PAD) + PAD]
            finish(c, mine, slice(c * HALF, (c + 1) * HALF))

    last.wait()
    for c in range(2):
        @pl.when(core == c)
        def _(c=c):
            finish(c, fin_recv[...], slice((1 - c) * HALF, (2 - c) * HALF))

    def drain(t, carry):
        for k in range(4):
            x_copy(t, k).wait_send()
        d_copy(t).wait_send()
        for k in range(3):
            for copy in y_copy(t, k):
                copy.wait_send()
        return carry

    lax.fori_loop(0, NZ, drain, 0)
    for t in range(NZ - 1):
        for copy in z_copy(t):
            copy.wait_send()


def on_device(mixed_heads, out_grads, admit_counts, lengths, gauss_noise):
    dma = pltpu.SemaphoreType.DMA
    bf16, i16 = jnp.bfloat16, jnp.int16
    inner, width = mixed_heads.shape[1], out_grads.shape[1]
    return pl.pallas_call(
        kernel,
        out_shape=jax.ShapeDtypeStruct(gauss_noise.shape, F32),
        in_specs=[
            pl.BlockSpec(memory_space=pltpu.SMEM),
            pl.BlockSpec(memory_space=pltpu.SMEM),
            pl.BlockSpec(memory_space=pl.ANY),
            pl.BlockSpec(memory_space=pl.ANY),
            pl.BlockSpec(memory_space=pltpu.VMEM),
        ],
        out_specs=pl.BlockSpec(memory_space=pltpu.VMEM),
        scratch_shapes=[
            pltpu.VMEM((NZ, NX * ROWS, CHUNK), bf16),
            pltpu.VMEM((ROWS, width), bf16),
            pltpu.VMEM((NX, ROWS, QUARTER), bf16),
            pltpu.VMEM((NX * ROWS, QUARTER), bf16),
            pltpu.VMEM((2, NY, HALF, QUARTER), F32),
            pltpu.VMEM((NZ, NY, HALF, QUARTER), F32),
            pltpu.VMEM((NZ, NY, HALF, QUARTER), F32),
            pltpu.VMEM((NZ, NY, HALF, QUARTER), F32),
            pltpu.VMEM((NZ, 3, HALF, QUARTER), i16),
            pltpu.VMEM((NZ, 3, 1, QUARTER), F32),
            pltpu.VMEM((NZ, 3, HALF, QUARTER), i16),
            pltpu.VMEM((NZ, 3, 1, QUARTER), F32),
            pltpu.VMEM((NZ - 1, HALF, QUARTER), i16),
            pltpu.VMEM((NZ - 1, 1, QUARTER), F32),
            pltpu.VMEM((NZ - 1, HALF, QUARTER), i16),
            pltpu.VMEM((NZ - 1, 1, QUARTER), F32),
            pltpu.VMEM((HALF, QUARTER), F32),
            pltpu.VMEM((HALF, PAD), F32),
            pltpu.VMEM((2, 14, 8, 128), jnp.int32),
            dma((NZ, NY)),
            dma,
            dma((NZ, 4)),
            dma((NZ, 4)),
            dma((3,)),
            dma((3,)),
            dma((NZ,)),
            dma((NZ,)),
            dma((NZ, 3)),
            dma((NZ, 3)),
            dma((NZ, 3)),
            dma((NZ, 3)),
            dma((NZ - 1,)),
            dma((NZ - 1,)),
            dma((NZ - 1,)),
            dma((NZ - 1,)),
            dma,
            dma,
            dma((14,)),
            dma((14,)),
        ],
        compiler_params=pltpu.CompilerParams(
            collective_id=0, has_side_effects=True, vmem_limit_bytes=63 * 1024 * 1024
        ),
        cost_estimate=pl.CostEstimate(flops=10**10, bytes_accessed=5 * 10**6, transcendentals=0),
    )(admit_counts, lengths, mixed_heads, out_grads, gauss_noise)


def solution(mesh):
    in_specs = (
        P(("dp", "fsdp"), None),
        P(("dp", "fsdp"), None),
        P(("dp", "fsdp")),
        P(("dp", "fsdp"), None),
        P("dp", "fsdp"),
    )
    return jax.shard_map(
        on_device, mesh=mesh, in_specs=in_specs, out_specs=P("dp", "fsdp"), check_vma=False
    )
```

```python
import functools

import jax
import jax.numpy as jnp
from jax import lax
from jax.experimental import pallas as pl
from jax.experimental.pallas import tpu as pltpu
from jax.sharding import PartitionSpec as P

MAXSEQ = 3
CLIP = 360000
MESH = pl.DeviceIdType.MESH
NX, NY, NZ = 4, 4, 8
ROWS = 240
FEW = 160
MOVED = 32
KEPT = ROWS - MOVED
CUT = 112
BLOCK = 128
CHUNK = NY * BLOCK
HALF = BLOCK // 2
SIDE = HALF // 2
QUARTER = 1152
WIDTH = 576
PAD = 640
F32 = jnp.float32


def quantise(value):
    top = jnp.maximum(jnp.max(jnp.abs(value), axis=0, keepdims=True), 1e-30)
    code = jnp.round(value * (32767.0 / top)).astype(jnp.int32).astype(jnp.int16)
    return code, top * (1.0 / 32767.0)


def restore(code, scale):
    return code.astype(jnp.int32).astype(F32) * scale


def kernel(
    count_ref, lengths_ref, x_hbm, g_hbm, noise_ref, out_ref,
    xraw, xmove, xs, graw, gcut, gs, part, near,
    asend, ascale, arecv, arscale, ysend, yscale, yrecv, yrscale,
    zsend, zscale, zrecv, zrscale, fin_send, full, turned, tally,
    load_sem, msend_sem, mrecv_sem, xsend_sem, xrecv_sem, gsend_sem, grecv_sem, dsend_sem, drecv_sem,
    asend_sem, arecv_sem, ysend_sem, yrecv_sem, zsend_sem, zrecv_sem,
    fsend_sem, frecv_sem, csend_sem, crecv_sem,
):
    dp = lax.axis_index("dp")
    fs = lax.axis_index("fsdp")
    x, core = fs // 2, fs % 2
    y, z = dp // NZ, dp % NZ

    def device(dx=0, dy=0, dz=0, dc=0):
        return (
            lax.rem(y + dy, NY) * NZ + lax.rem(z + dz, NZ),
            lax.rem(x + dx, NX) * 2 + lax.rem(core + dc, 2),
        )

    partners = (
        [device(dx=d) for d in (1, 2, 3)]
        + [device(dy=d) for d in (1, 2, 3)]
        + [device(dz=d) for d in range(1, NZ)]
        + [device(dc=1)]
    )
    barrier = pltpu.get_barrier_semaphore()
    for partner in partners:
        pl.semaphore_signal(barrier, inc=1, device_id=partner, device_id_type=MESH)

    x_load = pltpu.make_async_copy(x_hbm.at[pl.ds(0, ROWS)], xraw, load_sem.at[0])
    g_load = pltpu.make_async_copy(g_hbm.at[pl.ds(0, ROWS)], graw, load_sem.at[1])
    x_load.start()
    g_load.start()
    tally[0, 0] = jnp.full((8, 128), count_ref[0], jnp.int32)

    def target(t):
        return lax.rem(z + 1 + t, NZ)

    def remote(src, dst, send, recv, to):
        return pltpu.make_async_remote_copy(
            src_ref=src, dst_ref=dst, send_sem=send, recv_sem=recv, device_id=to, device_id_type=MESH
        )

    mate = device(dy=lax.rem(7 - 2 * y, NY))

    def move(k):
        if k == 2:
            src, dst = gcut.at[:, pl.ds(KEPT, MOVED)], gcut.at[:, pl.ds(FEW, MOVED)]
        else:
            steps = pl.ds(0, 2) if k == 0 else pl.ds(2, NZ - 2)
            src, dst = xmove.at[steps], xs.at[steps, pl.ds(FEW, MOVED)]
        return remote(src, dst, msend_sem.at[k], mrecv_sem.at[k], mate)

    def x_copy(t, k):
        if k == 0:
            src, dst, to = pl.ds(0, KEPT), pl.ds(KEPT, KEPT), device(dx=1)
        elif k == 1:
            src, dst, to = pl.ds(0, KEPT), pl.ds(2 * KEPT, KEPT), device(dx=3)
        elif k == 2:
            src, dst, to = pl.ds(KEPT, CUT), pl.ds(3 * KEPT, CUT), device(dx=1)
        else:
            src, dst, to = pl.ds(2 * KEPT + CUT, KEPT - CUT), pl.ds(3 * KEPT + CUT, KEPT - CUT), device(dx=3)
        return remote(xs.at[t, src], xs.at[t, dst], xsend_sem.at[t, k], xrecv_sem.at[t, k], to)

    def g_copy(k):
        d = (1, 3, 2)[k]
        return remote(
            gcut.at[lax.rem(x + d, NX), pl.ds(0, KEPT)], gs.at[pl.ds((k + 1) * KEPT, KEPT)],
            gsend_sem.at[k], grecv_sem.at[k], device(dx=d),
        )

    def d_copy(t):
        return remote(part.at[1 - core, t], near.at[t], dsend_sem.at[t], drecv_sem.at[t], device(dc=1))

    def a_copy(t, k):
        to = device(dy=(1, 3)[k])
        return (
            remote(asend.at[t, k], arecv.at[t, k], asend_sem.at[t, k, 0], arecv_sem.at[t, k, 0], to),
            remote(ascale.at[t, k], arscale.at[t, k], asend_sem.at[t, k, 1], arecv_sem.at[t, k, 1], to),
        )

    def y_copy(t, k):
        to = device(dy=(1, 3)[k])
        return (
            remote(ysend.at[t, k], yrecv.at[t, k], ysend_sem.at[t, k, 0], yrecv_sem.at[t, k, 0], to),
            remote(yscale.at[t, k], yrscale.at[t, k], ysend_sem.at[t, k, 1], yrecv_sem.at[t, k, 1], to),
        )

    def z_copy(t):
        to = device(dz=t + 1)
        return (
            remote(zsend.at[t], zrecv.at[t], zsend_sem.at[t, 0], zrecv_sem.at[t, 0], to),
            remote(zscale.at[t], zrscale.at[t], zsend_sem.at[t, 1], zrecv_sem.at[t, 1], to),
        )

    stages = (("dc", (1,)), ("dx", (1, 2, 3)), ("dy", (1, 2, 3)), ("dz", tuple(range(1, NZ))))
    first = (0, 1, 4, 7, 14)

    def c_copy(stage, i):
        axis, steps = stages[stage]
        slot = first[stage] + i
        return remote(
            tally.at[0, stage], tally.at[1, slot], csend_sem.at[slot], crecv_sem.at[slot], device(**{axis: steps[i]})
        )

    def count_send(stage):
        for i in range(len(stages[stage][1])):
            c_copy(stage, i).start()

    def count_take(stage):
        value = tally[0, stage]
        for i in range(len(stages[stage][1])):
            c_copy(stage, i).wait()
            value = value + tally[1, first[stage] + i]
        return value

    many = y >= NY // 2
    x_load.wait()

    def gather(t, carry):
        for j in range(NY):
            at = pl.multiple_of((j * NZ + target(t)) * BLOCK, BLOCK)
            to = slice(j * BLOCK, (j + 1) * BLOCK)
            xs[t, 0:FEW, to] = xraw[0:FEW, pl.ds(at, BLOCK)]
            xs[t, FEW + MOVED : KEPT, to] = xraw[FEW + MOVED : KEPT, pl.ds(at, BLOCK)]
            xmove[t, :, to] = xraw[KEPT:ROWS, pl.ds(at, BLOCK)]

            @pl.when(many)
            def _():
                xs[t, FEW : FEW + MOVED, to] = xraw[FEW : FEW + MOVED, pl.ds(at, BLOCK)]

        return carry

    lax.fori_loop(0, NZ, gather, 0)
    pl.semaphore_wait(barrier, len(partners))

    @pl.when(many)
    def _():
        move(0).start()
        move(1).start()

    count_send(0)

    @pl.when(jnp.logical_not(many))
    def _():
        move(0).wait_recv()

    for t in range(2):
        x_copy(t, 0).start()
        x_copy(t, 1).start()

    own = xraw[...]
    act = lax.dot_general(own, own, (((1,), (1,)), ((), ())), preferred_element_type=F32)
    g_load.wait()
    own = graw[...]
    grad = lax.dot_general(own, own, (((1,), (1,)), ((), ())), preferred_element_type=F32)
    product = act * grad
    row = lax.broadcasted_iota(jnp.int32, (ROWS, ROWS), 0)
    col = lax.broadcasted_iota(jnp.int32, (ROWS, ROWS), 1)
    line = lax.broadcasted_iota(jnp.int32, (ROWS, 1), 0)
    scale = jnp.zeros((ROWS, 1), F32)
    start = jnp.int32(0)
    for j in range(MAXSEQ):
        used = jnp.where(j < count_ref[0], lengths_ref[0, j], 0)
        end = start + used
        both = (row >= start) & (row < end) & (col >= start) & (col < end)
        sums = jnp.sum(jnp.where(both, product, 0.0), axis=1, keepdims=True)
        norm_sq = jnp.sum(sums, axis=0, keepdims=True)
        factor = CLIP / jnp.maximum(jnp.sqrt(norm_sq), F32(CLIP))
        scale = jnp.where((line >= start) & (line < end), factor, scale)
        start = end

    def clip(q, lo, hi):
        rows = graw[lo:hi, q * QUARTER : (q + 1) * QUARTER].astype(F32)
        gcut[q, lo:hi] = (scale[lo:hi] * rows).astype(jnp.bfloat16)

    for q in range(NX):
        clip(q, FEW + MOVED, ROWS)

    @pl.when(many)
    def _():
        move(2).start()
        for q in range(NX):
            clip(q, FEW, FEW + MOVED)

    for q in range(NX):
        clip(q, 0, FEW)

    for t in range(2):
        x_copy(t, 0).wait_recv()
        x_copy(t, 1).wait_recv()
        x_copy(t, 2).start()
        x_copy(t, 3).start()

    @pl.when(jnp.logical_not(many))
    def _():
        move(2).wait_recv()
        move(1).wait_recv()

    for k in range(3):
        g_copy(k).start()
    x_copy(2, 0).start()
    x_copy(2, 1).start()
    gs[0:KEPT] = gcut[x, 0:KEPT]

    def step(i, carry):
        @pl.when(i + 2 < NZ)
        def _():
            x_copy(i + 2, 0).start()
            x_copy(i + 2, 1).start()

        @pl.when((i >= 2) & (i < NZ))
        def _():
            x_copy(i, 0).wait_recv()
            x_copy(i, 1).wait_recv()
            x_copy(i, 2).start()
            x_copy(i, 3).start()

        @pl.when(i == 1)
        def _():
            for k in range(3):
                g_copy(k).wait()

        @pl.when(i < NZ + 1)
        def _():
            t = i - 1
            x_copy(t, 2).wait_recv()
            x_copy(t, 3).wait_recv()
            for pair in range(NY // 2):
                tile = lax.dot_general(
                    xs[t, :, pair * 2 * BLOCK : (pair + 1) * 2 * BLOCK], gs[...], (((0,), (0,)), ((), ())),
                    preferred_element_type=F32,
                )
                for k in range(2):
                    for h in range(2):
                        part[h, t, 2 * pair + k] = tile[k * BLOCK + h * HALF : k * BLOCK + (h + 1) * HALF]
            d_copy(t).start()

        for stage in range(4):
            @pl.when(i == 2 * stage + 1)
            def _(stage=stage):
                value = count_take(stage)
                tally[0, stage + 1] = value
                if stage < 3:
                    count_send(stage + 1)

        ahead, behind = lax.rem(y + 1, NY), lax.rem(y + 3, NY)
        far = lax.rem(y + 2, NY)

        @pl.when((i >= 2) & (i < NZ + 2))
        def _():
            t = i - 2
            d_copy(t).wait_recv()
            for k in range(2):
                rows = slice(k * SIDE, (k + 1) * SIDE)
                code, factor = quantise(part[core, t, far, rows] + near[t, far, rows])
                asend[t, k] = code
                ascale[t, k] = factor
                for copy in a_copy(t, k):
                    copy.start()

        @pl.when((i >= 3) & (i < NZ + 3))
        def _():
            t = i - 3
            for k in range(2):
                to = (ahead, behind)[k]
                value = part[core, t, to] + near[t, to]
                for copy in a_copy(t, k):
                    copy.wait_recv()
                more = restore(arecv[t, k], arscale[t, k])
                if k == 0:
                    value = jnp.concatenate([value[:SIDE] + more, value[SIDE:]], axis=0)
                else:
                    value = jnp.concatenate([value[:SIDE], value[SIDE:] + more], axis=0)
                code, factor = quantise(value)
                ysend[t, k] = code
                yscale[t, k] = factor
                for copy in y_copy(t, k):
                    copy.start()

        @pl.when(i >= 4)
        def _():
            t = i - 4
            value = part[core, t, y] + near[t, y]
            for k in range(2):
                for copy in y_copy(t, k):
                    copy.wait_recv()
                value += restore(yrecv[t, k], yrscale[t, k])

            @pl.when(t < NZ - 1)
            def _():
                code, factor = quantise(value)
                zsend[t] = code
                zscale[t] = factor
                for copy in z_copy(t):
                    copy.start()

            @pl.when(t == NZ - 1)
            def _():
                fin_send[...] = value

        return carry

    lax.fori_loop(1, NZ + 4, step, 0)

    value = fin_send[...]
    for t in range(NZ - 1):
        for copy in z_copy(t):
            copy.wait_recv()
        value += restore(zrecv[t], zrscale[t])
    fin_send[...] = value
    shift = QUARTER - PAD
    mine = pl.ds(pl.multiple_of(core * HALF, HALF), HALF)
    last = remote(
        fin_send.at[:, pl.ds(pl.multiple_of((1 - core) * shift, BLOCK), PAD)], full.at[mine], fsend_sem, frecv_sem,
        device(dc=1),
    )
    last.start()
    full[mine] = fin_send[:, pl.ds(pl.multiple_of(core * shift, BLOCK), PAD)]
    admitted = tally[0, 4, 0:1, 0:1].astype(F32)

    def drain(t, carry):
        for k in range(4):
            x_copy(t, k).wait_send()
        d_copy(t).wait_send()
        for k in range(2):
            for copy in a_copy(t, k) + y_copy(t, k):
                copy.wait_send()
        return carry

    lax.fori_loop(0, NZ, drain, 0)
    for t in range(NZ - 1):
        for copy in z_copy(t):
            copy.wait_send()

    @pl.when(many)
    def _():
        for k in range(3):
            move(k).wait_send()

    last.wait()
    turned[...] = jnp.transpose(full[...])
    lead = pl.multiple_of(core * (PAD - WIDTH), PAD - WIDTH)
    out_ref[...] = (turned[pl.ds(lead, WIDTH)] + noise_ref[...]) / admitted


def on_device(mixed_heads, out_grads, admit_counts, lengths, gauss_noise):
    dma = pltpu.SemaphoreType.DMA
    bf16, i16 = jnp.bfloat16, jnp.int16
    inner, width = mixed_heads.shape[1], out_grads.shape[1]
    turned = pl.pallas_call(
        kernel,
        out_shape=jax.ShapeDtypeStruct(gauss_noise.shape[::-1], F32),
        in_specs=[
            pl.BlockSpec(memory_space=pltpu.SMEM),
            pl.BlockSpec(memory_space=pltpu.SMEM),
            pl.BlockSpec(memory_space=pl.ANY),
            pl.BlockSpec(memory_space=pl.ANY),
            pl.BlockSpec(memory_space=pltpu.VMEM),
        ],
        out_specs=pl.BlockSpec(memory_space=pltpu.VMEM),
        scratch_shapes=[
            pltpu.VMEM((ROWS, inner), bf16),
            pltpu.VMEM((NZ, MOVED, CHUNK), bf16),
            pltpu.VMEM((NZ, NX * KEPT, CHUNK), bf16),
            pltpu.VMEM((ROWS, width), bf16),
            pltpu.VMEM((NX, ROWS, QUARTER), bf16),
            pltpu.VMEM((NX * KEPT, QUARTER), bf16),
            pltpu.VMEM((2, NZ, NY, HALF, QUARTER), F32),
            pltpu.VMEM((NZ, NY, HALF, QUARTER), F32),
            pltpu.VMEM((NZ, 2, SIDE, QUARTER), i16),
            pltpu.VMEM((NZ, 2, 1, QUARTER), F32),
            pltpu.VMEM((NZ, 2, SIDE, QUARTER), i16),
            pltpu.VMEM((NZ, 2, 1, QUARTER), F32),
            pltpu.VMEM((NZ, 2, HALF, QUARTER), i16),
            pltpu.VMEM((NZ, 2, 1, QUARTER), F32),
            pltpu.VMEM((NZ, 2, HALF, QUARTER), i16),
            pltpu.VMEM((NZ, 2, 1, QUARTER), F32),
            pltpu.VMEM((NZ - 1, HALF, QUARTER), i16),
            pltpu.VMEM((NZ - 1, 1, QUARTER), F32),
            pltpu.VMEM((NZ - 1, HALF, QUARTER), i16),
            pltpu.VMEM((NZ - 1, 1, QUARTER), F32),
            pltpu.VMEM((HALF, QUARTER), F32),
            pltpu.VMEM((BLOCK, PAD), F32),
            pltpu.VMEM((PAD, BLOCK), F32),
            pltpu.VMEM((2, 14, 8, 128), jnp.int32),
            dma((2,)),
            dma((3,)),
            dma((3,)),
            dma((NZ, 4)),
            dma((NZ, 4)),
            dma((3,)),
            dma((3,)),
            dma((NZ,)),
            dma((NZ,)),
            dma((NZ, 2, 2)),
            dma((NZ, 2, 2)),
            dma((NZ, 2, 2)),
            dma((NZ, 2, 2)),
            dma((NZ - 1, 2)),
            dma((NZ - 1, 2)),
            dma,
            dma,
            dma((14,)),
            dma((14,)),
        ],
        compiler_params=pltpu.CompilerParams(
            collective_id=0, has_side_effects=True, vmem_limit_bytes=63 * 1024 * 1024
        ),
        cost_estimate=pl.CostEstimate(flops=10**10, bytes_accessed=5 * 10**6, transcendentals=0),
    )(admit_counts, lengths, mixed_heads, out_grads, gauss_noise.T)
    return turned.T


def solution(mesh):
    in_specs = (
        P(("dp", "fsdp"), None),
        P(("dp", "fsdp"), None),
        P(("dp", "fsdp")),
        P(("dp", "fsdp"), None),
        P("dp", "fsdp"),
    )
    return jax.shard_map(
        on_device, mesh=mesh, in_specs=in_specs, out_specs=P("dp", "fsdp"), check_vma=False
    )
```

```python
import functools

import jax
import jax.numpy as jnp
from jax import lax
from jax.experimental import pallas as pl
from jax.experimental.pallas import tpu as pltpu
from jax.sharding import PartitionSpec as P

MAXSEQ = 3
CLIP = 360000
MESH = pl.DeviceIdType.MESH
NX, NY, NZ = 4, 4, 8
ROWS = 240
FEW = 160
MOVED = 32
KEPT = ROWS - MOVED
CUT = 112
BLOCK = 128
CHUNK = NY * BLOCK
HALF = BLOCK // 2
SIDE = HALF // 2
QUARTER = 1152
PARTS = 3
COLS = QUARTER // PARTS
UNITS = NZ * PARTS
SENT = UNITS - PARTS
WIDTH = 576
PAD = 640
F32 = jnp.float32


def quantise(value):
    top = jnp.maximum(jnp.max(jnp.abs(value), axis=0, keepdims=True), 1e-30)
    code = jnp.round(value * (32767.0 / top)).astype(jnp.int32).astype(jnp.int16)
    return code, top * (1.0 / 32767.0)


def restore(code, scale):
    return code.astype(jnp.int32).astype(F32) * scale


def kernel(
    count_ref, lengths_ref, x_hbm, g_hbm, noise_ref, out_ref,
    xraw, xmove, xs, graw, gcut, gs, part, near,
    asend, ascale, arecv, arscale, ysend, yscale, yrecv, yrscale,
    zsend, zscale, zrecv, zrscale, fin_send, full, turned, tally,
    load_sem, msend_sem, mrecv_sem, xsend_sem, xrecv_sem, gsend_sem, grecv_sem, dsend_sem, drecv_sem,
    asend_sem, arecv_sem, ysend_sem, yrecv_sem, zsend_sem, zrecv_sem,
    fsend_sem, frecv_sem, csend_sem, crecv_sem,
):
    dp = lax.axis_index("dp")
    fs = lax.axis_index("fsdp")
    x, core = fs // 2, fs % 2
    y, z = dp // NZ, dp % NZ

    def device(dx=0, dy=0, dz=0, dc=0):
        return (
            lax.rem(y + dy, NY) * NZ + lax.rem(z + dz, NZ),
            lax.rem(x + dx, NX) * 2 + lax.rem(core + dc, 2),
        )

    partners = (
        [device(dx=d) for d in (1, 2, 3)]
        + [device(dy=d) for d in (1, 2, 3)]
        + [device(dz=d) for d in range(1, NZ)]
        + [device(dc=1)]
    )
    barrier = pltpu.get_barrier_semaphore()
    for partner in partners:
        pl.semaphore_signal(barrier, inc=1, device_id=partner, device_id_type=MESH)

    x_load = pltpu.make_async_copy(x_hbm.at[pl.ds(0, ROWS)], xraw, load_sem.at[0])
    g_load = pltpu.make_async_copy(g_hbm.at[pl.ds(0, ROWS)], graw, load_sem.at[1])
    x_load.start()
    g_load.start()
    tally[0, 0] = jnp.full((8, 128), count_ref[0], jnp.int32)

    def target(t):
        return lax.rem(z + 1 + t, NZ)

    def remote(src, dst, send, recv, to):
        return pltpu.make_async_remote_copy(
            src_ref=src, dst_ref=dst, send_sem=send, recv_sem=recv, device_id=to, device_id_type=MESH
        )

    mate = device(dy=lax.rem(7 - 2 * y, NY))

    def move(k):
        if k == 2:
            src, dst = gcut.at[:, pl.ds(KEPT, MOVED)], gcut.at[:, pl.ds(FEW, MOVED)]
        else:
            steps = pl.ds(0, 2) if k == 0 else pl.ds(2, NZ - 2)
            src, dst = xmove.at[steps], xs.at[steps, pl.ds(FEW, MOVED)]
        return remote(src, dst, msend_sem.at[k], mrecv_sem.at[k], mate)

    def x_first(k, rest):
        lo, size = (FEW, KEPT - FEW) if rest else (0, FEW)
        to = device(dx=(1, 3)[k])
        sem = NZ if rest else 0
        return remote(
            xs.at[0, pl.ds(lo, size)], xs.at[0, pl.ds((k + 1) * KEPT + lo, size)], xsend_sem.at[sem, k],
            xrecv_sem.at[sem, k], to,
        )

    def x_copy(t, k):
        if k == 0:
            src, dst, to = pl.ds(0, KEPT), pl.ds(KEPT, KEPT), device(dx=1)
        elif k == 1:
            src, dst, to = pl.ds(0, KEPT), pl.ds(2 * KEPT, KEPT), device(dx=3)
        elif k == 2:
            src, dst, to = pl.ds(KEPT, CUT), pl.ds(3 * KEPT, CUT), device(dx=1)
        else:
            src, dst, to = pl.ds(2 * KEPT + CUT, KEPT - CUT), pl.ds(3 * KEPT + CUT, KEPT - CUT), device(dx=3)
        return remote(xs.at[t, src], xs.at[t, dst], xsend_sem.at[t, k], xrecv_sem.at[t, k], to)

    def g_copy(k):
        d = (1, 3, 2)[k]
        return remote(
            gcut.at[lax.rem(x + d, NX), pl.ds(0, KEPT)], gs.at[pl.ds((k + 1) * KEPT, KEPT)],
            gsend_sem.at[k], grecv_sem.at[k], device(dx=d),
        )

    def d_copy(u):
        return remote(part.at[1 - core, u], near.at[u], dsend_sem.at[u], drecv_sem.at[u], device(dc=1))

    def a_copy(t, k):
        to = device(dy=(1, 3)[k])
        return (
            remote(asend.at[t, k], arecv.at[t, k], asend_sem.at[t, k, 0], arecv_sem.at[t, k, 0], to),
            remote(ascale.at[t, k], arscale.at[t, k], asend_sem.at[t, k, 1], arecv_sem.at[t, k, 1], to),
        )

    def y_copy(t, k):
        to = device(dy=(1, 3)[k])
        return (
            remote(ysend.at[t, k], yrecv.at[t, k], ysend_sem.at[t, k, 0], yrecv_sem.at[t, k, 0], to),
            remote(yscale.at[t, k], yrscale.at[t, k], ysend_sem.at[t, k, 1], yrecv_sem.at[t, k, 1], to),
        )

    def z_copy(t):
        to = device(dz=t // PARTS + 1)
        return (
            remote(zsend.at[t], zrecv.at[t], zsend_sem.at[t, 0], zrecv_sem.at[t, 0], to),
            remote(zscale.at[t], zrscale.at[t], zsend_sem.at[t, 1], zrecv_sem.at[t, 1], to),
        )

    stages = (("dc", (1,)), ("dx", (1, 2, 3)), ("dy", (1, 2, 3)), ("dz", tuple(range(1, NZ))))
    first = (0, 1, 4, 7, 14)

    def c_copy(stage, i):
        axis, steps = stages[stage]
        slot = first[stage] + i
        return remote(
            tally.at[0, stage], tally.at[1, slot], csend_sem.at[slot], crecv_sem.at[slot], device(**{axis: steps[i]})
        )

    def count_send(stage):
        for i in range(len(stages[stage][1])):
            c_copy(stage, i).start()

    def count_take(stage):
        value = tally[0, stage]
        for i in range(len(stages[stage][1])):
            c_copy(stage, i).wait()
            value = value + tally[1, first[stage] + i]
        return value

    many = y >= NY // 2
    x_load.wait()

    def block(t, j):
        return pl.ds(pl.multiple_of((j * NZ + target(t)) * BLOCK, BLOCK), BLOCK)

    def gather(t, carry):
        for j in range(NY):
            to = slice(j * BLOCK, (j + 1) * BLOCK)
            xs[t, 0:FEW, to] = xraw[0:FEW, block(t, j)]
            xs[t, FEW + MOVED : KEPT, to] = xraw[FEW + MOVED : KEPT, block(t, j)]

            @pl.when(many)
            def _():
                xs[t, FEW : FEW + MOVED, to] = xraw[FEW : FEW + MOVED, block(t, j)]

        return carry

    def hand(t, carry):
        for j in range(NY):
            xmove[t, :, j * BLOCK : (j + 1) * BLOCK] = xraw[KEPT:ROWS, block(t, j)]
        return carry

    @pl.when(many)
    def _():
        lax.fori_loop(0, NZ, hand, 0)

    gather(0, 0)
    pl.semaphore_wait(barrier, len(partners))

    @pl.when(many)
    def _():
        move(0).start()

    x_first(0, False).start()
    x_first(1, False).start()

    @pl.when(many)
    def _():
        move(1).start()

    lax.fori_loop(1, NZ, gather, 0)
    count_send(0)

    @pl.when(jnp.logical_not(many))
    def _():
        move(0).wait_recv()

    x_first(0, True).start()
    x_first(1, True).start()
    x_copy(1, 0).start()
    x_copy(1, 1).start()

    own = xraw[...]
    act = lax.dot_general(own, own, (((1,), (1,)), ((), ())), preferred_element_type=F32)
    g_load.wait()
    own = graw[...]
    grad = lax.dot_general(own, own, (((1,), (1,)), ((), ())), preferred_element_type=F32)
    product = act * grad
    row = lax.broadcasted_iota(jnp.int32, (ROWS, ROWS), 0)
    col = lax.broadcasted_iota(jnp.int32, (ROWS, ROWS), 1)
    line = lax.broadcasted_iota(jnp.int32, (ROWS, 1), 0)
    scale = jnp.zeros((ROWS, 1), F32)
    start = jnp.int32(0)
    for j in range(MAXSEQ):
        used = jnp.where(j < count_ref[0], lengths_ref[0, j], 0)
        end = start + used
        both = (row >= start) & (row < end) & (col >= start) & (col < end)
        sums = jnp.sum(jnp.where(both, product, 0.0), axis=1, keepdims=True)
        norm_sq = jnp.sum(sums, axis=0, keepdims=True)
        factor = CLIP / jnp.maximum(jnp.sqrt(norm_sq), F32(CLIP))
        scale = jnp.where((line >= start) & (line < end), factor, scale)
        start = end

    def clip(q, lo, hi):
        rows = graw[lo:hi, q * QUARTER : (q + 1) * QUARTER].astype(F32)
        gcut[q, lo:hi] = (scale[lo:hi] * rows).astype(jnp.bfloat16)

    for q in range(NX):
        clip(q, FEW + MOVED, ROWS)

    @pl.when(many)
    def _():
        move(2).start()
        for q in range(NX):
            clip(q, FEW, FEW + MOVED)

    for q in range(NX):
        clip(q, 0, FEW)

    for k in range(2):
        x_first(k, False).wait_recv()
        x_first(k, True).wait_recv()
    x_copy(0, 2).start()
    x_copy(0, 3).start()

    @pl.when(jnp.logical_not(many))
    def _():
        move(1).wait_recv()

    x_copy(2, 0).start()
    x_copy(2, 1).start()
    x_copy(1, 0).wait_recv()
    x_copy(1, 1).wait_recv()
    x_copy(1, 2).start()
    x_copy(1, 3).start()

    @pl.when(jnp.logical_not(many))
    def _():
        move(2).wait_recv()

    for k in range(3):
        g_copy(k).start()
    x_copy(3, 0).start()
    x_copy(3, 1).start()
    gs[0:KEPT] = gcut[x, 0:KEPT]
    fin_send[...] = jnp.zeros((HALF, QUARTER), F32)
    x_copy(2, 0).wait_recv()
    x_copy(2, 1).wait_recv()
    x_copy(2, 2).start()
    x_copy(2, 3).start()
    x_copy(4, 0).start()
    x_copy(4, 1).start()
    for k in range(3):
        g_copy(k).wait()

    ahead, behind = lax.rem(y + 1, NY), lax.rem(y + 3, NY)
    far = lax.rem(y + 2, NY)

    def columns(u):
        return pl.ds(pl.multiple_of((u % PARTS) * COLS, BLOCK), COLS)

    def step(i, carry):
        begin = i % PARTS == 0
        now = i // PARTS

        @pl.when(begin & (now >= 2) & (now + 1 < NZ))
        def _():
            t = now + 1
            x_copy(t, 0).wait_recv()
            x_copy(t, 1).wait_recv()
            x_copy(t, 2).start()
            x_copy(t, 3).start()

            @pl.when(t + 2 < NZ)
            def _():
                x_copy(t + 2, 0).start()
                x_copy(t + 2, 1).start()

        @pl.when(begin & (now < NZ))
        def _():
            t = now
            x_copy(t, 2).wait_recv()
            x_copy(t, 3).wait_recv()
            for pair in range(NY // 2):
                tile = lax.dot_general(
                    xs[t, :, pair * 2 * BLOCK : (pair + 1) * 2 * BLOCK], gs[...], (((0,), (0,)), ((), ())),
                    preferred_element_type=F32,
                )
                for k in range(2):
                    for h in range(2):
                        rows = slice(k * BLOCK + h * HALF, k * BLOCK + (h + 1) * HALF)
                        for n in range(PARTS):
                            part[h, t * PARTS + n, 2 * pair + k] = tile[rows, n * COLS : (n + 1) * COLS]
            for n in range(PARTS):
                d_copy(t * PARTS + n).start()

        for stage in range(4):
            @pl.when(i == 4 * stage + 1)
            def _(stage=stage):
                value = count_take(stage)
                tally[0, stage + 1] = value
                if stage < 3:
                    count_send(stage + 1)

        @pl.when((i >= 1) & (i < UNITS + 1))
        def _():
            u = i - 1
            d_copy(u).wait_recv()
            for k in range(2):
                rows = slice(k * SIDE, (k + 1) * SIDE)
                code, factor = quantise(part[core, u, far, rows] + near[u, far, rows])
                asend[u, k] = code
                ascale[u, k] = factor
                for copy in a_copy(u, k):
                    copy.start()

        @pl.when((i >= 3) & (i < UNITS + 3))
        def _():
            u = i - 3
            for k in range(2):
                to = (ahead, behind)[k]
                value = part[core, u, to] + near[u, to]
                for copy in a_copy(u, k):
                    copy.wait_recv()
                more = restore(arecv[u, k], arscale[u, k])
                if k == 0:
                    value = jnp.concatenate([value[:SIDE] + more, value[SIDE:]], axis=0)
                else:
                    value = jnp.concatenate([value[:SIDE], value[SIDE:] + more], axis=0)
                code, factor = quantise(value)
                ysend[u, k] = code
                yscale[u, k] = factor
                for copy in y_copy(u, k):
                    copy.start()

        @pl.when((i >= 5) & (i < UNITS + 5))
        def _():
            u = i - 5
            value = part[core, u, y] + near[u, y]
            for k in range(2):
                for copy in y_copy(u, k):
                    copy.wait_recv()
                value += restore(yrecv[u, k], yrscale[u, k])

            @pl.when(u < SENT)
            def _():
                code, factor = quantise(value)
                zsend[u] = code
                zscale[u] = factor
                for copy in z_copy(u):
                    copy.start()

            @pl.when(u >= SENT)
            def _():
                fin_send[:, columns(u)] += value

        @pl.when(i >= 9)
        def _():
            u = i - 9
            for copy in z_copy(u):
                copy.wait_recv()
            fin_send[:, columns(u)] += restore(zrecv[u], zrscale[u])

        @pl.when((i >= 8) & (i < UNITS + 6))
        def _():
            sent(i - 8)

        @pl.when(begin & (now >= 3))
        def _():
            for k in range(4):
                x_copy(now - 2, k).wait_send()

        return carry

    def sent(u):
        d_copy(u).wait_send()
        for k in range(2):
            for copy in a_copy(u, k) + y_copy(u, k):
                copy.wait_send()

        @pl.when(u < SENT)
        def _():
            for copy in z_copy(u):
                copy.wait_send()

    lax.fori_loop(0, UNITS + 6, step, 0)

    shift = QUARTER - PAD
    mine = pl.ds(pl.multiple_of(core * HALF, HALF), HALF)
    last = remote(
        fin_send.at[:, pl.ds(pl.multiple_of((1 - core) * shift, BLOCK), PAD)], full.at[mine], fsend_sem, frecv_sem,
        device(dc=1),
    )
    last.start()
    full[mine] = fin_send[:, pl.ds(pl.multiple_of(core * shift, BLOCK), PAD)]
    admitted = tally[0, 4, 0:1, 0:1].astype(F32)

    for u in (UNITS - 2, UNITS - 1):
        sent(u)
    for k in range(2):
        x_first(k, False).wait_send()
        x_first(k, True).wait_send()
        x_copy(0, 2 + k).wait_send()

    @pl.when(many)
    def _():
        for k in range(3):
            move(k).wait_send()

    last.wait()
    turned[...] = jnp.transpose(full[...])
    lead = pl.multiple_of(core * (PAD - WIDTH), PAD - WIDTH)
    out_ref[...] = (turned[pl.ds(lead, WIDTH)] + noise_ref[...]) / admitted


def on_device(mixed_heads, out_grads, admit_counts, lengths, gauss_noise):
    dma = pltpu.SemaphoreType.DMA
    bf16, i16 = jnp.bfloat16, jnp.int16
    inner, width = mixed_heads.shape[1], out_grads.shape[1]
    turned = pl.pallas_call(
        kernel,
        out_shape=jax.ShapeDtypeStruct(gauss_noise.shape[::-1], F32),
        in_specs=[
            pl.BlockSpec(memory_space=pltpu.SMEM),
            pl.BlockSpec(memory_space=pltpu.SMEM),
            pl.BlockSpec(memory_space=pl.ANY),
            pl.BlockSpec(memory_space=pl.ANY),
            pl.BlockSpec(memory_space=pltpu.VMEM),
        ],
        out_specs=pl.BlockSpec(memory_space=pltpu.VMEM),
        scratch_shapes=[
            pltpu.VMEM((ROWS, inner), bf16),
            pltpu.VMEM((NZ, MOVED, CHUNK), bf16),
            pltpu.VMEM((NZ, NX * KEPT, CHUNK), bf16),
            pltpu.VMEM((ROWS, width), bf16),
            pltpu.VMEM((NX, ROWS, QUARTER), bf16),
            pltpu.VMEM((NX * KEPT, QUARTER), bf16),
            pltpu.VMEM((2, UNITS, NY, HALF, COLS), F32),
            pltpu.VMEM((UNITS, NY, HALF, COLS), F32),
            pltpu.VMEM((UNITS, 2, SIDE, COLS), i16),
            pltpu.VMEM((UNITS, 2, 1, COLS), F32),
            pltpu.VMEM((UNITS, 2, SIDE, COLS), i16),
            pltpu.VMEM((UNITS, 2, 1, COLS), F32),
            pltpu.VMEM((UNITS, 2, HALF, COLS), i16),
            pltpu.VMEM((UNITS, 2, 1, COLS), F32),
            pltpu.VMEM((UNITS, 2, HALF, COLS), i16),
            pltpu.VMEM((UNITS, 2, 1, COLS), F32),
            pltpu.VMEM((SENT, HALF, COLS), i16),
            pltpu.VMEM((SENT, 1, COLS), F32),
            pltpu.VMEM((SENT, HALF, COLS), i16),
            pltpu.VMEM((SENT, 1, COLS), F32),
            pltpu.VMEM((HALF, QUARTER), F32),
            pltpu.VMEM((BLOCK, PAD), F32),
            pltpu.VMEM((PAD, BLOCK), F32),
            pltpu.VMEM((2, 14, 8, 128), jnp.int32),
            dma((2,)),
            dma((3,)),
            dma((3,)),
            dma((NZ + 1, 4)),
            dma((NZ + 1, 4)),
            dma((3,)),
            dma((3,)),
            dma((UNITS,)),
            dma((UNITS,)),
            dma((UNITS, 2, 2)),
            dma((UNITS, 2, 2)),
            dma((UNITS, 2, 2)),
            dma((UNITS, 2, 2)),
            dma((SENT, 2)),
            dma((SENT, 2)),
            dma,
            dma,
            dma((14,)),
            dma((14,)),
        ],
        compiler_params=pltpu.CompilerParams(
            collective_id=0, has_side_effects=True, vmem_limit_bytes=63 * 1024 * 1024
        ),
        cost_estimate=pl.CostEstimate(flops=10**10, bytes_accessed=5 * 10**6, transcendentals=0),
    )(admit_counts, lengths, mixed_heads, out_grads, gauss_noise.T)
    return turned.T


def solution(mesh):
    in_specs = (
        P(("dp", "fsdp"), None),
        P(("dp", "fsdp"), None),
        P(("dp", "fsdp")),
        P(("dp", "fsdp"), None),
        P("dp", "fsdp"),
    )
    return jax.shard_map(
        on_device, mesh=mesh, in_specs=in_specs, out_specs=P("dp", "fsdp"), check_vma=False
    )
```

```python
import functools

import jax
import jax.numpy as jnp
from jax import lax
from jax.experimental import pallas as pl
from jax.experimental.pallas import tpu as pltpu
from jax.sharding import PartitionSpec as P

MAXSEQ = 3
CLIP = 360000
MESH = pl.DeviceIdType.MESH
NX, NY, NZ = 4, 4, 8
ROWS = 240
FEW = 160
MOVED = 32
KEPT = ROWS - MOVED
CUT = 112
BLOCK = 128
CHUNK = NY * BLOCK
HALF = BLOCK // 2
SIDE = HALF // 2
QUARTER = 1152
LAST = NZ - 1
ENDING = NZ - 2
ORDER = (2, 1, 3, 0)
TAIL = (((6, 0), (7, 0)), ((6, 1), (6, 2)), ((7, 1), (7, 2)), ((6, 3), (7, 3)))
WIDTH = 576
PAD = 640
F32 = jnp.float32


def quantise(value):
    top = jnp.maximum(jnp.max(jnp.abs(value), axis=0, keepdims=True), 1e-30)
    code = jnp.round(value * (32767.0 / top)).astype(jnp.int32).astype(jnp.int16)
    return code, top * (1.0 / 32767.0)


def restore(code, scale):
    return code.astype(jnp.int32).astype(F32) * scale


def kernel(
    count_ref, lengths_ref, x_hbm, g_hbm, noise_hbm, out_ref,
    xraw, xmove, xs, graw, gcut, gs, noise, part, near,
    asend, ascale, arecv, arscale, ysend, yscale, yrecv, yrscale,
    zsend, zscale, zrecv, zrscale, fin_send, full, turned, tally,
    load_sem, msend_sem, mrecv_sem, xsend_sem, xrecv_sem, gsend_sem, grecv_sem, dsend_sem, drecv_sem,
    asend_sem, arecv_sem, ysend_sem, yrecv_sem, zsend_sem, zrecv_sem,
    fsend_sem, frecv_sem, csend_sem, crecv_sem,
):
    dp = lax.axis_index("dp")
    fs = lax.axis_index("fsdp")
    x, core = fs // 2, fs % 2
    y, z = dp // NZ, dp % NZ
    one = 1 + 2 * core
    two = NX - one

    def device(dx=0, dy=0, dz=0, dc=0):
        return (
            lax.rem(y + dy, NY) * NZ + lax.rem(z + dz, NZ),
            lax.rem(x + dx, NX) * 2 + lax.rem(core + dc, 2),
        )

    partners = (
        [device(dx=d) for d in (1, 2, 3)]
        + [device(dy=d) for d in (1, 2, 3)]
        + [device(dz=d) for d in range(1, NZ)]
        + [device(dc=1)]
    )
    barrier = pltpu.get_barrier_semaphore()
    for partner in partners:
        pl.semaphore_signal(barrier, inc=1, device_id=partner, device_id_type=MESH)

    x_load = pltpu.make_async_copy(x_hbm.at[pl.ds(0, ROWS)], xraw, load_sem.at[0])
    g_load = pltpu.make_async_copy(g_hbm.at[pl.ds(0, ROWS)], graw, load_sem.at[1])
    n_load = pltpu.make_async_copy(noise_hbm, noise, load_sem.at[2])
    x_load.start()
    g_load.start()
    n_load.start()
    tally[0, 0] = jnp.full((8, 128), count_ref[0], jnp.int32)

    def away(t):
        odd = t % 2
        return (1 - odd) * (NZ // 2 - t // 2) + odd * (NZ // 2 + 1 + t // 2)

    def target(t):
        return lax.rem(z + away(t), NZ)

    def remote(src, dst, send, recv, to):
        return pltpu.make_async_remote_copy(
            src_ref=src, dst_ref=dst, send_sem=send, recv_sem=recv, device_id=to, device_id_type=MESH
        )

    mate = device(dy=lax.rem(7 - 2 * y, NY))

    def move(k):
        if k == 2:
            src, dst = gcut.at[:, pl.ds(KEPT, MOVED)], gcut.at[:, pl.ds(FEW, MOVED)]
        else:
            steps = pl.ds(0, 2) if k == 0 else pl.ds(2, NZ - 2)
            src, dst = xmove.at[steps], xs.at[steps, pl.ds(FEW, MOVED)]
        return remote(src, dst, msend_sem.at[k], mrecv_sem.at[k], mate)

    def x_rows(k):
        if k == 0:
            return pl.ds(0, KEPT), pl.ds(KEPT, KEPT), device(dx=one)
        if k == 1:
            return pl.ds(0, KEPT), pl.ds(2 * KEPT, KEPT), device(dx=two)
        if k == 2:
            return pl.ds(KEPT, CUT), pl.ds(3 * KEPT, CUT), device(dx=one)
        return pl.ds(2 * KEPT + CUT, KEPT - CUT), pl.ds(3 * KEPT + CUT, KEPT - CUT), device(dx=two)

    def x_first(k, rest):
        lo, size = (FEW, KEPT - FEW) if rest else (0, FEW)
        sem = NZ + 2 if rest else 0
        return remote(
            xs.at[0, pl.ds(lo, size)], xs.at[0, pl.ds((k + 1) * KEPT + lo, size)], xsend_sem.at[sem, k],
            xrecv_sem.at[sem, k], device(dx=(one, two)[k]),
        )

    def x_copy(t, k):
        src, dst, to = x_rows(k)
        return remote(xs.at[t, src], xs.at[t, dst], xsend_sem.at[t, k], xrecv_sem.at[t, k], to)

    def x_half(h, k):
        src, dst, to = x_rows(k)
        t, cols = ENDING + h // 2, pl.ds((h % 2) * 2 * BLOCK, 2 * BLOCK)
        return remote(
            xs.at[t, src, cols], xs.at[t, dst, cols], xsend_sem.at[ENDING + h, k], xrecv_sem.at[ENDING + h, k], to
        )

    def g_copy(k, rest):
        d = (one, two, 2)[k]
        lo, size = (FEW, KEPT - FEW) if rest else (0, FEW)
        return remote(
            gcut.at[lax.rem(x + d, NX), pl.ds(lo, size)], gs.at[pl.ds((k + 1) * KEPT + lo, size)],
            gsend_sem.at[k, rest], grecv_sem.at[k, rest], device(dx=d),
        )

    def d_piece(t, p):
        return remote(
            part.at[1 - core, t, p], near.at[t, p], dsend_sem.at[t, p], drecv_sem.at[t, p], device(dc=1)
        )

    def d_copy(t, pair):
        two_of = pl.ds(2 * pair, 2)
        return remote(
            part.at[1 - core, t, two_of], near.at[t, two_of], dsend_sem.at[t, pair], drecv_sem.at[t, pair], device(dc=1)
        )

    def a_copy(t, k):
        to = device(dy=(1, 3)[k])
        return (
            remote(asend.at[t, k], arecv.at[t, k], asend_sem.at[t, k, 0], arecv_sem.at[t, k, 0], to),
            remote(ascale.at[t, k], arscale.at[t, k], asend_sem.at[t, k, 1], arecv_sem.at[t, k, 1], to),
        )

    def y_copy(t, k):
        to = device(dy=(1, 3)[k])
        return (
            remote(ysend.at[t, k], yrecv.at[t, k], ysend_sem.at[t, k, 0], yrecv_sem.at[t, k, 0], to),
            remote(yscale.at[t, k], yrscale.at[t, k], ysend_sem.at[t, k, 1], yrecv_sem.at[t, k, 1], to),
        )

    def z_copy(t):
        to = device(dz=away(t))
        return (
            remote(zsend.at[t], zrecv.at[t], zsend_sem.at[t, 0], zrecv_sem.at[t, 0], to),
            remote(zscale.at[t], zrscale.at[t], zsend_sem.at[t, 1], zrecv_sem.at[t, 1], to),
        )

    stages = (("dc", (1,)), ("dx", (1, 2, 3)), ("dy", (1, 2, 3)), ("dz", tuple(range(1, NZ))))
    first = (0, 1, 4, 7, 14)

    def c_copy(stage, i):
        axis, steps = stages[stage]
        slot = first[stage] + i
        return remote(
            tally.at[0, stage], tally.at[1, slot], csend_sem.at[slot], crecv_sem.at[slot], device(**{axis: steps[i]})
        )

    def count_send(stage):
        for i in range(len(stages[stage][1])):
            c_copy(stage, i).start()

    def count_take(stage):
        value = tally[0, stage]
        for i in range(len(stages[stage][1])):
            c_copy(stage, i).wait()
            value = value + tally[1, first[stage] + i]
        return value

    many = y >= NY // 2
    x_load.wait()

    def block(t, j, owner=y):
        if isinstance(t, int) and t >= ENDING:
            t, j = TAIL[2 * (t - ENDING) + j // 2][j % 2]
        return pl.ds(pl.multiple_of((lax.rem(owner + ORDER[j], NY) * NZ + target(t)) * BLOCK, BLOCK), BLOCK)

    def gather(t, carry):
        for j in range(NY):
            to = slice(j * BLOCK, (j + 1) * BLOCK)
            xs[t, 0:FEW, to] = xraw[0:FEW, block(t, j)]
            xs[t, FEW + MOVED : KEPT, to] = xraw[FEW + MOVED : KEPT, block(t, j)]

            @pl.when(many)
            def _():
                xs[t, FEW : FEW + MOVED, to] = xraw[FEW : FEW + MOVED, block(t, j)]

        return carry

    def hand(t, carry):
        for j in range(NY):
            xmove[t, :, j * BLOCK : (j + 1) * BLOCK] = xraw[KEPT:ROWS, block(t, j, NY - 1 - y)]
        return carry

    @pl.when(many)
    def _():
        lax.fori_loop(0, ENDING, hand, 0)
        for t in range(ENDING, NZ):
            hand(t, 0)

    gather(0, 0)
    pl.semaphore_wait(barrier, len(partners))

    @pl.when(many)
    def _():
        move(0).start()

    x_first(0, False).start()
    x_first(1, False).start()

    @pl.when(many)
    def _():
        move(1).start()

    gather(1, 0)
    count_send(0)

    @pl.when(jnp.logical_not(many))
    def _():
        move(0).wait_recv()

    x_first(0, True).start()
    x_first(1, True).start()
    x_copy(1, 0).start()
    x_copy(1, 1).start()

    own = xraw[...]
    act = lax.dot_general(own, own, (((1,), (1,)), ((), ())), preferred_element_type=F32)
    g_load.wait()
    own = graw[...]
    grad = lax.dot_general(own, own, (((1,), (1,)), ((), ())), preferred_element_type=F32)
    product = act * grad
    row = lax.broadcasted_iota(jnp.int32, (ROWS, ROWS), 0)
    col = lax.broadcasted_iota(jnp.int32, (ROWS, ROWS), 1)
    line = lax.broadcasted_iota(jnp.int32, (ROWS, 1), 0)
    scale = jnp.zeros((ROWS, 1), F32)
    start = jnp.int32(0)
    for j in range(MAXSEQ):
        used = jnp.where(j < count_ref[0], lengths_ref[0, j], 0)
        end = start + used
        both = (row >= start) & (row < end) & (col >= start) & (col < end)
        sums = jnp.sum(jnp.where(both, product, 0.0), axis=1, keepdims=True)
        norm_sq = jnp.sum(sums, axis=0, keepdims=True)
        factor = CLIP / jnp.maximum(jnp.sqrt(norm_sq), F32(CLIP))
        scale = jnp.where((line >= start) & (line < end), factor, scale)
        start = end

    def clip(q, lo, hi):
        rows = graw[lo:hi, pl.ds(pl.multiple_of(q * QUARTER, BLOCK), QUARTER)].astype(F32)
        gcut[q, lo:hi] = (scale[lo:hi] * rows).astype(jnp.bfloat16)

    for q in range(NX):
        clip(q, FEW + MOVED, ROWS)

    @pl.when(many)
    def _():
        move(2).start()

    for d in range(NX):
        clip(lax.rem(x + 1 + d, NX), 0, FEW)
    for k in range(3):
        g_copy(k, 0).start()

    @pl.when(many)
    def _():
        for q in range(NX):
            clip(q, FEW, FEW + MOVED)
        for k in range(3):
            g_copy(k, 1).start()

    for k in range(2):
        x_first(k, False).wait_recv()
        x_first(k, True).wait_recv()
    x_copy(0, 2).start()
    x_copy(0, 3).start()

    @pl.when(jnp.logical_not(many))
    def _():
        move(2).wait_recv()
        for k in range(3):
            g_copy(k, 1).start()

    lax.fori_loop(2, ENDING, gather, 0)
    for t in range(ENDING, NZ):
        gather(t, 0)
    gs[0:KEPT] = gcut[x, 0:KEPT]
    fin_send[...] = jnp.zeros((HALF, QUARTER), F32)

    @pl.when(jnp.logical_not(many))
    def _():
        move(1).wait_recv()

    x_copy(1, 0).wait_recv()
    x_copy(1, 1).wait_recv()
    x_copy(1, 2).start()
    x_copy(1, 3).start()
    for k in range(3):
        g_copy(k, 0).wait_recv()
    x_copy(2, 0).start()
    x_copy(2, 1).start()
    for k in range(3):
        g_copy(k, 1).wait_recv()
    x_copy(3, 0).start()
    x_copy(3, 1).start()

    def multiply(t, pair, pieces):
        cols = slice(pair * 2 * BLOCK, (pair + 1) * 2 * BLOCK)
        tile = lax.dot_general(xs[t, :, cols], gs[...], (((0,), (0,)), ((), ())), preferred_element_type=F32)
        for k in range(2):
            for h in range(2):
                part[h, pieces[k][0], pieces[k][1]] = tile[k * BLOCK + h * HALF : k * BLOCK + (h + 1) * HALF]

    def spread(t):
        for k in range(2):
            rows = slice(k * SIDE, (k + 1) * SIDE)
            code, factor = quantise(part[core, t, 0, rows] + near[t, 0, rows])
            asend[t, k] = code
            ascale[t, k] = factor
            for copy in a_copy(t, k):
                copy.start()

    def pass_on(t, k):
        value = part[core, t, 1 + k] + near[t, 1 + k]
        for copy in a_copy(t, k):
            copy.wait_recv()
        more = restore(arecv[t, k], arscale[t, k])
        if k == 0:
            value = jnp.concatenate([value[:SIDE] + more, value[SIDE:]], axis=0)
        else:
            value = jnp.concatenate([value[:SIDE], value[SIDE:] + more], axis=0)
        code, factor = quantise(value)
        ysend[t, k] = code
        yscale[t, k] = factor
        for copy in y_copy(t, k):
            copy.start()

    def collect(t):
        value = part[core, t, 3] + near[t, 3]
        for k in range(2):
            for copy in y_copy(t, k):
                copy.wait_recv()
            value += restore(yrecv[t, k], yrscale[t, k])
        return value

    def deliver(t):
        code, factor = quantise(collect(t))
        zsend[t] = code
        zscale[t] = factor
        for copy in z_copy(t):
            copy.start()

    def accept(t):
        for copy in z_copy(t):
            copy.wait_recv()
        fin_send[...] += restore(zrecv[t], zrscale[t])

    def sent(t):
        for k in range(2):
            for copy in a_copy(t, k) + y_copy(t, k):
                copy.wait_send()

    def product(t):
        x_copy(t, 2).wait_recv()
        x_copy(t, 3).wait_recv()
        for pair in range(2):
            multiply(t, pair, ((t, 2 * pair), (t, 2 * pair + 1)))
            d_copy(t, pair).start()

    def onward(t):
        d_copy(t, 1).wait_recv()
        pass_on(t, 0)
        pass_on(t, 1)

    def step(t, carry):
        @pl.when(t >= 1)
        def _():
            i = t + 1
            x_copy(i, 0).wait_recv()
            x_copy(i, 1).wait_recv()
            x_copy(i, 2).start()
            x_copy(i, 3).start()

            @pl.when(t <= 2)
            def _():
                x_copy(t + 3, 0).start()
                x_copy(t + 3, 1).start()

            @pl.when(t == 3)
            def _():
                for h in range(2):
                    for k in range(2):
                        x_half(h, k).start()

            @pl.when(t == 4)
            def _():
                for k in range(2):
                    x_half(2, k).start()

        product(t)

        for stage in range(4):
            @pl.when(t == stage + 1)
            def _(stage=stage):
                value = count_take(stage)
                tally[0, stage + 1] = value
                if stage < 3:
                    count_send(stage + 1)

        d_copy(t, 0).wait_recv()
        spread(t)

        @pl.when(t >= 1)
        def _():
            onward(t - 1)

        @pl.when(t >= 2)
        def _():
            deliver(t - 2)

        @pl.when(t >= 3)
        def _():
            sent(t - 3)
            for k in range(4):
                x_copy(t - 2, k).wait_send()

        return carry

    lax.fori_loop(0, ENDING - 1, step, 0)

    def forward(h):
        for k in range(2):
            x_half(h, k).wait_recv()
        for k in range(2):
            x_half(h, k + 2).start()

    def produce(h):
        for k in range(2):
            x_half(h, k + 2).wait_recv()
        multiply(ENDING + h // 2, h % 2, TAIL[h])
        for t, p in TAIL[h]:
            d_piece(t, p).start()

    def hand_out(t, p):
        d_piece(t, p).wait_recv()
        if p == 0:
            spread(t)
        elif p < 3:
            pass_on(t, p - 1)

    t = ENDING - 1
    forward(0)
    for k in range(2):
        x_half(3, k).start()
    product(t)
    forward(1)
    d_copy(t, 0).wait_recv()
    spread(t)
    onward(t - 1)
    deliver(t - 2)
    forward(2)
    produce(0)
    onward(t)
    hand_out(6, 0)
    hand_out(7, 0)
    deliver(t - 1)
    produce(1)
    forward(3)
    hand_out(6, 1)
    hand_out(6, 2)
    produce(2)
    deliver(t)
    hand_out(7, 1)
    hand_out(7, 2)
    produce(3)
    hand_out(6, 3)
    deliver(6)
    for i in range(LAST - 1):
        accept(i)
    hand_out(7, 3)
    fin_send[...] += collect(LAST)
    accept(LAST - 1)
    shift = QUARTER - PAD
    mine = pl.ds(pl.multiple_of(core * HALF, HALF), HALF)
    last = remote(
        fin_send.at[:, pl.ds(pl.multiple_of((1 - core) * shift, BLOCK), PAD)], full.at[mine], fsend_sem, frecv_sem,
        device(dc=1),
    )
    last.start()
    full[mine] = fin_send[:, pl.ds(pl.multiple_of(core * shift, BLOCK), PAD)]
    admitted = tally[0, 4, 0:1, 0:1].astype(F32)

    for k in range(4):
        for h in range(4):
            x_half(h, k).wait_send()
        for i in range(ENDING - 3, ENDING):
            x_copy(i, k).wait_send()
    for k in range(2):
        x_first(k, False).wait_send()
        x_first(k, True).wait_send()
        x_copy(0, 2 + k).wait_send()
    for i in range(ENDING):
        for pair in range(2):
            d_copy(i, pair).wait_send()
    for i in range(ENDING, NZ):
        for p in range(4):
            d_piece(i, p).wait_send()
    for i in range(ENDING - 4, NZ):
        sent(i)
    for i in range(LAST):
        for copy in z_copy(i):
            copy.wait_send()

    @pl.when(many)
    def _():
        for k in range(3):
            move(k).wait_send()

    n_load.wait()
    for k in range(3):
        for rest in range(2):
            g_copy(k, rest).wait_send()
    last.wait()
    turned[...] = jnp.transpose(full[...])
    lead = pl.multiple_of(core * (PAD - WIDTH), PAD - WIDTH)
    out_ref[...] = (turned[pl.ds(lead, WIDTH)] + noise[...]) / admitted


def on_device(mixed_heads, out_grads, admit_counts, lengths, gauss_noise):
    dma = pltpu.SemaphoreType.DMA
    bf16, i16 = jnp.bfloat16, jnp.int16
    inner, width = mixed_heads.shape[1], out_grads.shape[1]
    turned = pl.pallas_call(
        kernel,
        out_shape=jax.ShapeDtypeStruct(gauss_noise.shape[::-1], F32),
        in_specs=[
            pl.BlockSpec(memory_space=pltpu.SMEM),
            pl.BlockSpec(memory_space=pltpu.SMEM),
            pl.BlockSpec(memory_space=pl.ANY),
            pl.BlockSpec(memory_space=pl.ANY),
            pl.BlockSpec(memory_space=pl.ANY),
        ],
        out_specs=pl.BlockSpec(memory_space=pltpu.VMEM),
        scratch_shapes=[
            pltpu.VMEM((ROWS, inner), bf16),
            pltpu.VMEM((NZ, MOVED, CHUNK), bf16),
            pltpu.VMEM((NZ, NX * KEPT, CHUNK), bf16),
            pltpu.VMEM((ROWS, width), bf16),
            pltpu.VMEM((NX, ROWS, QUARTER), bf16),
            pltpu.VMEM((NX * KEPT, QUARTER), bf16),
            pltpu.VMEM(gauss_noise.shape[::-1], F32),
            pltpu.VMEM((2, NZ, NY, HALF, QUARTER), F32),
            pltpu.VMEM((NZ, NY, HALF, QUARTER), F32),
            pltpu.VMEM((NZ, 2, SIDE, QUARTER), i16),
            pltpu.VMEM((NZ, 2, 1, QUARTER), F32),
            pltpu.VMEM((NZ, 2, SIDE, QUARTER), i16),
            pltpu.VMEM((NZ, 2, 1, QUARTER), F32),
            pltpu.VMEM((NZ, 2, HALF, QUARTER), i16),
            pltpu.VMEM((NZ, 2, 1, QUARTER), F32),
            pltpu.VMEM((NZ, 2, HALF, QUARTER), i16),
            pltpu.VMEM((NZ, 2, 1, QUARTER), F32),
            pltpu.VMEM((LAST, HALF, QUARTER), i16),
            pltpu.VMEM((LAST, 1, QUARTER), F32),
            pltpu.VMEM((LAST, HALF, QUARTER), i16),
            pltpu.VMEM((LAST, 1, QUARTER), F32),
            pltpu.VMEM((HALF, QUARTER), F32),
            pltpu.VMEM((BLOCK, PAD), F32),
            pltpu.VMEM((PAD, BLOCK), F32),
            pltpu.VMEM((2, 14, 8, 128), jnp.int32),
            dma((3,)),
            dma((3,)),
            dma((3,)),
            dma((NZ + 3, 4)),
            dma((NZ + 3, 4)),
            dma((3, 2)),
            dma((3, 2)),
            dma((NZ, 4)),
            dma((NZ, 4)),
            dma((NZ, 2, 2)),
            dma((NZ, 2, 2)),
            dma((NZ, 2, 2)),
            dma((NZ, 2, 2)),
            dma((LAST, 2)),
            dma((LAST, 2)),
            dma,
            dma,
            dma((14,)),
            dma((14,)),
        ],
        compiler_params=pltpu.CompilerParams(
            collective_id=0, has_side_effects=True, vmem_limit_bytes=63 * 1024 * 1024
        ),
        cost_estimate=pl.CostEstimate(flops=10**10, bytes_accessed=5 * 10**6, transcendentals=0),
    )(admit_counts, lengths, mixed_heads, out_grads, gauss_noise.T)
    return turned.T


def solution(mesh):
    in_specs = (
        P(("dp", "fsdp"), None),
        P(("dp", "fsdp"), None),
        P(("dp", "fsdp")),
        P(("dp", "fsdp"), None),
        P("dp", "fsdp"),
    )
    return jax.shard_map(
        on_device, mesh=mesh, in_specs=in_specs, out_specs=P("dp", "fsdp"), check_vma=False
    )
```

```python
import functools

import jax
import jax.numpy as jnp
from jax import lax
from jax.experimental import pallas as pl
from jax.experimental.pallas import tpu as pltpu
from jax.sharding import PartitionSpec as P

MAXSEQ = 3
CLIP = 360000
MESH = pl.DeviceIdType.MESH
NX, NY, NZ = 4, 4, 8
ROWS = 240
FEW = 160
MOVED = 32
KEPT = ROWS - MOVED
CUT = 112
BLOCK = 128
CHUNK = NY * BLOCK
HALF = BLOCK // 2
SIDE = HALF // 2
QUARTER = 1152
LAST = NZ - 1
ENDING = NZ - 2
ORDER = (2, 1, 3, 0)
TAIL = (((6, 0), (7, 0)), ((6, 1), (6, 2)), ((7, 1), (7, 2)), ((6, 3), (7, 3)))
WIDTH = 576
PAD = 640
F32 = jnp.float32


def quantise(value):
    top = jnp.maximum(jnp.max(jnp.abs(value), axis=0, keepdims=True), 1e-30)
    code = jnp.round(value * (32767.0 / top)).astype(jnp.int32).astype(jnp.int16)
    return code, top * (1.0 / 32767.0)


def restore(code, scale):
    return code.astype(jnp.int32).astype(F32) * scale


def kernel(
    count_ref, lengths_ref, x_hbm, g_hbm, noise_hbm, out_ref,
    xraw, xmove, xs, graw, gcut, gs, noise, part, near,
    asend, ascale, arecv, arscale, ysend, yscale, yrecv, yrscale,
    zsend, zscale, zrecv, zrscale, fin_send, full, turned, tally,
    load_sem, msend_sem, mrecv_sem, xsend_sem, xrecv_sem, gsend_sem, grecv_sem, dsend_sem, drecv_sem,
    asend_sem, arecv_sem, ysend_sem, yrecv_sem, zsend_sem, zrecv_sem,
    fsend_sem, frecv_sem, csend_sem, crecv_sem,
):
    dp = lax.axis_index("dp")
    fs = lax.axis_index("fsdp")
    x, core = fs // 2, fs % 2
    y, z = dp // NZ, dp % NZ
    one = 1 + 2 * core
    two = NX - one

    def device(dx=0, dy=0, dz=0, dc=0):
        return (
            lax.rem(y + dy, NY) * NZ + lax.rem(z + dz, NZ),
            lax.rem(x + dx, NX) * 2 + lax.rem(core + dc, 2),
        )

    partners = (
        [device(dx=d) for d in (1, 2, 3)]
        + [device(dy=d) for d in (1, 2, 3)]
        + [device(dz=d) for d in range(1, NZ)]
        + [device(dc=1)]
    )
    barrier = pltpu.get_barrier_semaphore()
    for partner in partners:
        pl.semaphore_signal(barrier, inc=1, device_id=partner, device_id_type=MESH)

    x_load = pltpu.make_async_copy(x_hbm.at[pl.ds(0, ROWS)], xraw, load_sem.at[0])
    g_load = pltpu.make_async_copy(g_hbm.at[pl.ds(0, ROWS)], graw, load_sem.at[1])
    n_load = pltpu.make_async_copy(noise_hbm, noise, load_sem.at[2])
    x_load.start()
    g_load.start()
    n_load.start()
    tally[0, 0] = jnp.full((8, 128), count_ref[0], jnp.int32)

    def away(t):
        odd = t % 2
        return (1 - odd) * (NZ // 2 - t // 2) + odd * (NZ // 2 + 1 + t // 2)

    def target(t):
        return lax.rem(z + away(t), NZ)

    def remote(src, dst, send, recv, to):
        return pltpu.make_async_remote_copy(
            src_ref=src, dst_ref=dst, send_sem=send, recv_sem=recv, device_id=to, device_id_type=MESH
        )

    mate = device(dy=lax.rem(7 - 2 * y, NY))

    def move(k):
        if k == 2:
            src, dst = gcut.at[:, pl.ds(KEPT, MOVED)], gcut.at[:, pl.ds(FEW, MOVED)]
        else:
            steps = pl.ds(0, 2) if k == 0 else pl.ds(2, NZ - 2)
            src, dst = xmove.at[steps], xs.at[steps, pl.ds(FEW, MOVED)]
        return remote(src, dst, msend_sem.at[k], mrecv_sem.at[k], mate)

    def x_rows(k):
        if k == 0:
            return pl.ds(0, KEPT), pl.ds(KEPT, KEPT), device(dx=one)
        if k == 1:
            return pl.ds(0, KEPT), pl.ds(2 * KEPT, KEPT), device(dx=two)
        if k == 2:
            return pl.ds(KEPT, CUT), pl.ds(3 * KEPT, CUT), device(dx=one)
        return pl.ds(2 * KEPT + CUT, KEPT - CUT), pl.ds(3 * KEPT + CUT, KEPT - CUT), device(dx=two)

    def x_first(k, rest):
        lo, size = (FEW, KEPT - FEW) if rest else (0, FEW)
        sem = NZ + 2 if rest else 0
        return remote(
            xs.at[0, pl.ds(lo, size)], xs.at[0, pl.ds((k + 1) * KEPT + lo, size)], xsend_sem.at[sem, k],
            xrecv_sem.at[sem, k], device(dx=(one, two)[k]),
        )

    def x_copy(t, k):
        src, dst, to = x_rows(k)
        return remote(xs.at[t, src], xs.at[t, dst], xsend_sem.at[t, k], xrecv_sem.at[t, k], to)

    def x_half(h, k):
        src, dst, to = x_rows(k)
        t, cols = ENDING + h // 2, pl.ds((h % 2) * 2 * BLOCK, 2 * BLOCK)
        return remote(
            xs.at[t, src, cols], xs.at[t, dst, cols], xsend_sem.at[ENDING + h, k], xrecv_sem.at[ENDING + h, k], to
        )

    def g_copy(k, rest):
        d = (one, two, 2)[k]
        lo, size = (FEW, KEPT - FEW) if rest else (0, FEW)
        return remote(
            gcut.at[lax.rem(x + d, NX), pl.ds(lo, size)], gs.at[pl.ds((k + 1) * KEPT + lo, size)],
            gsend_sem.at[k, rest], grecv_sem.at[k, rest], device(dx=d),
        )

    def d_piece(t, p):
        return remote(
            part.at[1 - core, t, p], near.at[t, p], dsend_sem.at[t, p], drecv_sem.at[t, p], device(dc=1)
        )

    def d_copy(t, pair):
        two_of = pl.ds(2 * pair, 2)
        return remote(
            part.at[1 - core, t, two_of], near.at[t, two_of], dsend_sem.at[t, pair], drecv_sem.at[t, pair], device(dc=1)
        )

    def a_copy(t, k):
        to = device(dy=(1, 3)[k])
        return (
            remote(asend.at[t, k], arecv.at[t, k], asend_sem.at[t, k, 0], arecv_sem.at[t, k, 0], to),
            remote(ascale.at[t, k], arscale.at[t, k], asend_sem.at[t, k, 1], arecv_sem.at[t, k, 1], to),
        )

    def y_copy(t, k):
        to = device(dy=(1, 3)[k])
        return (
            remote(ysend.at[t, k], yrecv.at[t, k], ysend_sem.at[t, k, 0], yrecv_sem.at[t, k, 0], to),
            remote(yscale.at[t, k], yrscale.at[t, k], ysend_sem.at[t, k, 1], yrecv_sem.at[t, k, 1], to),
        )

    def z_copy(t):
        to = device(dz=away(t))
        return (
            remote(zsend.at[t], zrecv.at[t], zsend_sem.at[t, 0], zrecv_sem.at[t, 0], to),
            remote(zscale.at[t], zrscale.at[t], zsend_sem.at[t, 1], zrecv_sem.at[t, 1], to),
        )

    stages = (("dc", (1,)), ("dx", (1, 2, 3)), ("dy", (1, 2, 3)), ("dz", tuple(range(1, NZ))))
    first = (0, 1, 4, 7, 14)

    def c_copy(stage, i):
        axis, steps = stages[stage]
        slot = first[stage] + i
        return remote(
            tally.at[0, stage], tally.at[1, slot], csend_sem.at[slot], crecv_sem.at[slot], device(**{axis: steps[i]})
        )

    def count_send(stage):
        for i in range(len(stages[stage][1])):
            c_copy(stage, i).start()

    def count_take(stage):
        value = tally[0, stage]
        for i in range(len(stages[stage][1])):
            c_copy(stage, i).wait()
            value = value + tally[1, first[stage] + i]
        return value

    many = y >= NY // 2
    x_load.wait()

    def block(t, j, owner=y):
        if isinstance(t, int) and t >= ENDING:
            t, j = TAIL[2 * (t - ENDING) + j // 2][j % 2]
        return pl.ds(pl.multiple_of((lax.rem(owner + ORDER[j], NY) * NZ + target(t)) * BLOCK, BLOCK), BLOCK)

    def gather(t, carry):
        for j in range(NY):
            to = slice(j * BLOCK, (j + 1) * BLOCK)
            xs[t, 0:FEW, to] = xraw[0:FEW, block(t, j)]
            xs[t, FEW + MOVED : KEPT, to] = xraw[FEW + MOVED : KEPT, block(t, j)]

            @pl.when(many)
            def _():
                xs[t, FEW : FEW + MOVED, to] = xraw[FEW : FEW + MOVED, block(t, j)]

        return carry

    def hand(t, carry):
        for j in range(NY):
            xmove[t, :, j * BLOCK : (j + 1) * BLOCK] = xraw[KEPT:ROWS, block(t, j, NY - 1 - y)]
        return carry

    @pl.when(many)
    def _():
        lax.fori_loop(0, ENDING, hand, 0)
        for t in range(ENDING, NZ):
            hand(t, 0)

    gather(0, 0)
    pl.semaphore_wait(barrier, len(partners))

    @pl.when(many)
    def _():
        move(0).start()

    x_first(0, False).start()
    x_first(1, False).start()

    @pl.when(many)
    def _():
        move(1).start()

    gather(1, 0)
    count_send(0)

    @pl.when(jnp.logical_not(many))
    def _():
        move(0).wait_recv()

    x_first(0, True).start()
    x_first(1, True).start()
    x_copy(1, 0).start()
    x_copy(1, 1).start()

    own = xraw[...]
    act = lax.dot_general(own, own, (((1,), (1,)), ((), ())), preferred_element_type=F32)
    g_load.wait()
    own = graw[...]
    grad = lax.dot_general(own, own, (((1,), (1,)), ((), ())), preferred_element_type=F32)
    product = act * grad
    row = lax.broadcasted_iota(jnp.int32, (ROWS, ROWS), 0)
    col = lax.broadcasted_iota(jnp.int32, (ROWS, ROWS), 1)
    line = lax.broadcasted_iota(jnp.int32, (ROWS, 1), 0)
    scale = jnp.zeros((ROWS, 1), F32)
    start = jnp.int32(0)
    for j in range(MAXSEQ):
        used = jnp.where(j < count_ref[0], lengths_ref[0, j], 0)
        end = start + used
        both = (row >= start) & (row < end) & (col >= start) & (col < end)
        sums = jnp.sum(jnp.where(both, product, 0.0), axis=1, keepdims=True)
        norm_sq = jnp.sum(sums, axis=0, keepdims=True)
        factor = CLIP / jnp.maximum(jnp.sqrt(norm_sq), F32(CLIP))
        scale = jnp.where((line >= start) & (line < end), factor, scale)
        start = end

    def clip(q, lo, hi):
        rows = graw[lo:hi, pl.ds(pl.multiple_of(q * QUARTER, BLOCK), QUARTER)].astype(F32)
        gcut[q, lo:hi] = (scale[lo:hi] * rows).astype(jnp.bfloat16)

    for q in range(NX):
        clip(q, FEW + MOVED, ROWS)

    @pl.when(many)
    def _():
        move(2).start()

    for d in range(NX):
        clip(lax.rem(x + 1 + d, NX), 0, FEW)
    for k in range(3):
        g_copy(k, 0).start()

    @pl.when(many)
    def _():
        for q in range(NX):
            clip(q, FEW, FEW + MOVED)
        for k in range(3):
            g_copy(k, 1).start()

    for k in range(2):
        x_first(k, False).wait_recv()
        x_first(k, True).wait_recv()
    x_copy(0, 2).start()
    x_copy(0, 3).start()

    @pl.when(jnp.logical_not(many))
    def _():
        move(2).wait_recv()
        for k in range(3):
            g_copy(k, 1).start()

    lax.fori_loop(2, ENDING, gather, 0)
    for t in range(ENDING, NZ):
        gather(t, 0)
    gs[0:KEPT] = gcut[x, 0:KEPT]
    fin_send[...] = jnp.zeros((HALF, QUARTER), F32)

    @pl.when(jnp.logical_not(many))
    def _():
        move(1).wait_recv()

    x_copy(1, 0).wait_recv()
    x_copy(1, 1).wait_recv()
    x_copy(1, 2).start()
    x_copy(1, 3).start()
    for k in range(3):
        g_copy(k, 0).wait_recv()
    x_copy(2, 0).start()
    x_copy(2, 1).start()
    for k in range(3):
        g_copy(k, 1).wait_recv()
    x_copy(3, 0).start()
    x_copy(3, 1).start()

    def multiply(t, pair, pieces):
        cols = slice(pair * 2 * BLOCK, (pair + 1) * 2 * BLOCK)
        tile = lax.dot_general(xs[t, :, cols], gs[...], (((0,), (0,)), ((), ())), preferred_element_type=F32)
        for k in range(2):
            for h in range(2):
                part[h, pieces[k][0], pieces[k][1]] = tile[k * BLOCK + h * HALF : k * BLOCK + (h + 1) * HALF]

    def spread(t):
        for k in range(2):
            rows = slice(k * SIDE, (k + 1) * SIDE)
            code, factor = quantise(part[core, t, 0, rows] + near[t, 0, rows])
            asend[t, k] = code
            ascale[t, k] = factor
            for copy in a_copy(t, k):
                copy.start()

    def pass_on(t, k):
        value = part[core, t, 1 + k] + near[t, 1 + k]
        for copy in a_copy(t, k):
            copy.wait_recv()
        more = restore(arecv[t, k], arscale[t, k])
        if k == 0:
            value = jnp.concatenate([value[:SIDE] + more, value[SIDE:]], axis=0)
        else:
            value = jnp.concatenate([value[:SIDE], value[SIDE:] + more], axis=0)
        code, factor = quantise(value)
        ysend[t, k] = code
        yscale[t, k] = factor
        for copy in y_copy(t, k):
            copy.start()

    def collect(t):
        value = part[core, t, 3] + near[t, 3]
        for k in range(2):
            for copy in y_copy(t, k):
                copy.wait_recv()
            value += restore(yrecv[t, k], yrscale[t, k])
        return value

    def deliver(t):
        code, factor = quantise(collect(t))
        zsend[t] = code
        zscale[t] = factor
        for copy in z_copy(t):
            copy.start()

    def accept(t):
        for copy in z_copy(t):
            copy.wait_recv()
        fin_send[...] += restore(zrecv[t], zrscale[t])

    def sent(t):
        for k in range(2):
            for copy in a_copy(t, k) + y_copy(t, k):
                copy.wait_send()

    def product(t):
        x_copy(t, 2).wait_recv()
        x_copy(t, 3).wait_recv()
        for pair in range(2):
            multiply(t, pair, ((t, 2 * pair), (t, 2 * pair + 1)))
            d_copy(t, pair).start()

    def onward(t):
        d_copy(t, 1).wait_recv()
        pass_on(t, 0)
        pass_on(t, 1)

    def step(t, carry):
        @pl.when(t >= 1)
        def _():
            i = t + 1
            x_copy(i, 0).wait_recv()
            x_copy(i, 1).wait_recv()
            x_copy(i, 2).start()
            x_copy(i, 3).start()

            @pl.when(t <= 2)
            def _():
                x_copy(t + 3, 0).start()
                x_copy(t + 3, 1).start()

            @pl.when(t == 3)
            def _():
                for h in range(2):
                    for k in range(2):
                        x_half(h, k).start()

            @pl.when(t == 4)
            def _():
                for k in range(2):
                    x_half(2, k).start()

        product(t)

        for stage in range(4):
            @pl.when(t == stage + 1)
            def _(stage=stage):
                value = count_take(stage)
                tally[0, stage + 1] = value
                if stage < 3:
                    count_send(stage + 1)

        d_copy(t, 0).wait_recv()
        spread(t)

        @pl.when(t >= 2)
        def _():
            deliver(t - 2)

        @pl.when(t >= 1)
        def _():
            onward(t - 1)

        @pl.when(t >= 3)
        def _():
            sent(t - 3)
            for k in range(4):
                x_copy(t - 2, k).wait_send()

        return carry

    lax.fori_loop(0, ENDING - 1, step, 0)

    def forward(h):
        for k in range(2):
            x_half(h, k).wait_recv()
        for k in range(2):
            x_half(h, k + 2).start()

    def produce(h):
        for k in range(2):
            x_half(h, k + 2).wait_recv()
        multiply(ENDING + h // 2, h % 2, TAIL[h])
        for t, p in TAIL[h]:
            d_piece(t, p).start()

    def hand_out(t, p):
        d_piece(t, p).wait_recv()
        if p == 0:
            spread(t)
        elif p < 3:
            pass_on(t, p - 1)

    t = ENDING - 1
    forward(0)
    for k in range(2):
        x_half(3, k).start()
    product(t)
    forward(1)
    d_copy(t, 0).wait_recv()
    spread(t)
    onward(t - 1)
    deliver(t - 2)
    forward(2)
    produce(0)
    onward(t)
    hand_out(6, 0)
    hand_out(7, 0)
    deliver(t - 1)
    produce(1)
    forward(3)
    hand_out(6, 1)
    hand_out(6, 2)
    produce(2)
    deliver(t)
    hand_out(7, 1)
    hand_out(7, 2)
    produce(3)
    hand_out(6, 3)
    deliver(6)
    for i in range(LAST - 2):
        accept(i)
    for k in range(4):
        for h in range(4):
            x_half(h, k).wait_send()
        for i in range(ENDING - 3, ENDING):
            x_copy(i, k).wait_send()
    for k in range(2):
        x_first(k, False).wait_send()
        x_first(k, True).wait_send()
        x_copy(0, 2 + k).wait_send()
    for i in range(ENDING):
        for pair in range(2):
            d_copy(i, pair).wait_send()
    for p in range(4):
        d_piece(ENDING, p).wait_send()
    for i in range(ENDING - 4, LAST):
        sent(i)
    for i in range(LAST - 1):
        for copy in z_copy(i):
            copy.wait_send()
    for k in range(3):
        for rest in range(2):
            g_copy(k, rest).wait_send()

    @pl.when(many)
    def _():
        for k in range(3):
            move(k).wait_send()

    hand_out(7, 3)
    accept(LAST - 2)
    fin_send[...] += collect(LAST)
    accept(LAST - 1)
    shift = QUARTER - PAD
    mine = pl.ds(pl.multiple_of(core * HALF, HALF), HALF)
    last = remote(
        fin_send.at[:, pl.ds(pl.multiple_of((1 - core) * shift, BLOCK), PAD)], full.at[mine], fsend_sem, frecv_sem,
        device(dc=1),
    )
    last.start()
    full[mine] = fin_send[:, pl.ds(pl.multiple_of(core * shift, BLOCK), PAD)]
    admitted = tally[0, 4, 0:1, 0:1].astype(F32)

    for copy in z_copy(LAST - 1):
        copy.wait_send()
    sent(LAST)
    for p in range(4):
        d_piece(LAST, p).wait_send()
    n_load.wait()
    last.wait()
    turned[...] = jnp.transpose(full[...])
    lead = pl.multiple_of(core * (PAD - WIDTH), PAD - WIDTH)
    out_ref[...] = (turned[pl.ds(lead, WIDTH)] + noise[...]) / admitted


def on_device(mixed_heads, out_grads, admit_counts, lengths, gauss_noise):
    dma = pltpu.SemaphoreType.DMA
    bf16, i16 = jnp.bfloat16, jnp.int16
    inner, width = mixed_heads.shape[1], out_grads.shape[1]
    turned = pl.pallas_call(
        kernel,
        out_shape=jax.ShapeDtypeStruct(gauss_noise.shape[::-1], F32),
        in_specs=[
            pl.BlockSpec(memory_space=pltpu.SMEM),
            pl.BlockSpec(memory_space=pltpu.SMEM),
            pl.BlockSpec(memory_space=pl.ANY),
            pl.BlockSpec(memory_space=pl.ANY),
            pl.BlockSpec(memory_space=pl.ANY),
        ],
        out_specs=pl.BlockSpec(memory_space=pltpu.VMEM),
        scratch_shapes=[
            pltpu.VMEM((ROWS, inner), bf16),
            pltpu.VMEM((NZ, MOVED, CHUNK), bf16),
            pltpu.VMEM((NZ, NX * KEPT, CHUNK), bf16),
            pltpu.VMEM((ROWS, width), bf16),
            pltpu.VMEM((NX, ROWS, QUARTER), bf16),
            pltpu.VMEM((NX * KEPT, QUARTER), bf16),
            pltpu.VMEM(gauss_noise.shape[::-1], F32),
            pltpu.VMEM((2, NZ, NY, HALF, QUARTER), F32),
            pltpu.VMEM((NZ, NY, HALF, QUARTER), F32),
            pltpu.VMEM((NZ, 2, SIDE, QUARTER), i16),
            pltpu.VMEM((NZ, 2, 1, QUARTER), F32),
            pltpu.VMEM((NZ, 2, SIDE, QUARTER), i16),
            pltpu.VMEM((NZ, 2, 1, QUARTER), F32),
            pltpu.VMEM((NZ, 2, HALF, QUARTER), i16),
            pltpu.VMEM((NZ, 2, 1, QUARTER), F32),
            pltpu.VMEM((NZ, 2, HALF, QUARTER), i16),
            pltpu.VMEM((NZ, 2, 1, QUARTER), F32),
            pltpu.VMEM((LAST, HALF, QUARTER), i16),
            pltpu.VMEM((LAST, 1, QUARTER), F32),
            pltpu.VMEM((LAST, HALF, QUARTER), i16),
            pltpu.VMEM((LAST, 1, QUARTER), F32),
            pltpu.VMEM((HALF, QUARTER), F32),
            pltpu.VMEM((BLOCK, PAD), F32),
            pltpu.VMEM((PAD, BLOCK), F32),
            pltpu.VMEM((2, 14, 8, 128), jnp.int32),
            dma((3,)),
            dma((3,)),
            dma((3,)),
            dma((NZ + 3, 4)),
            dma((NZ + 3, 4)),
            dma((3, 2)),
            dma((3, 2)),
            dma((NZ, 4)),
            dma((NZ, 4)),
            dma((NZ, 2, 2)),
            dma((NZ, 2, 2)),
            dma((NZ, 2, 2)),
            dma((NZ, 2, 2)),
            dma((LAST, 2)),
            dma((LAST, 2)),
            dma,
            dma,
            dma((14,)),
            dma((14,)),
        ],
        compiler_params=pltpu.CompilerParams(
            collective_id=0, has_side_effects=True, vmem_limit_bytes=63 * 1024 * 1024
        ),
        cost_estimate=pl.CostEstimate(flops=10**10, bytes_accessed=5 * 10**6, transcendentals=0),
    )(admit_counts, lengths, mixed_heads, out_grads, gauss_noise.T)
    return turned.T


def solution(mesh):
    in_specs = (
        P(("dp", "fsdp"), None),
        P(("dp", "fsdp"), None),
        P(("dp", "fsdp")),
        P(("dp", "fsdp"), None),
        P("dp", "fsdp"),
    )
    return jax.shard_map(
        on_device, mesh=mesh, in_specs=in_specs, out_specs=P("dp", "fsdp"), check_vma=False
    )
```
